32 devices in a mesh: row: 4 (over y, core), col: 8 (over z, x).
Axes of the slice: x: 2, y: 2, z: 4, core: 2. Of those that a mesh axis runs over, the one named last changes fastest.
Arguments:
- descriptors: bfloat16 [2048, 1024], P(('row', 'col'))
- gradients: bfloat16 [3, 4, 2048, 1024], P(None, None, ('row', 'col'))
- sparse_panel: bfloat16 [512, 1024], P('col')
- sparse_trail: bfloat16 [1024, 1024], P('col')
- atom_counts: int32 [32, 4], P(('row', 'col')), may hold values from 1 to 16, 32 in all within a row
- owner_rows: int32 [32, 4], P(('row', 'col')), may hold values from 0 to 3, each once within a row
- neighbor_ids: int32 [128, 16, 4], P(('row', 'col')), may hold values from 0 to 65519
Outputs:
- panel_factor: float32 [512, 512], replicated
- cross_factor: float32 [1024, 512], P('col')
- trail_residual: float32 [1024, 8192], P('col', 'row')
The draws below stay inside these ranges and needn't reach their ends.
Inputs may be any that keep to these rules, and one draw needn't show every extreme that they name: `atom_counts`: the structures of one device's line hold 32 atoms together, and every line has a structure of 16 atoms. `owner_rows`: every device gives exactly one structure to each row group.
All inputs are finite; a program needn't handle non-finite values.
Results may differ from the reference program's by a relative error of at most 0.0043.
Values may be sent and summed in bfloat16 or wider, within the bound.
A program may use at most 128 MiB of HBM per device.

```python
import math
import jax
import jax.numpy as jnp
import numpy as np
from jax import lax

DESC = 1024
PANEL = 512
AMAX = 16
NEIGH = 4
STRUCT_DEV = 4
STRUCTS = 128
ATOM_DEV = 32
ATOMS = 2048
ROWS = 8192
TRAIL = 1024
N_ROW = 4
N_COL = 8
DEVICES = 32


def shared_center(key):
    center = jax.random.truncated_normal(jax.random.fold_in(key, 11), -4.0, 4.0, (DESC,), jnp.float32)
    return center * DESC ** (-0.25)


def rough_noise(key, array_shape):
    return jax.random.truncated_normal(key, -4.0, 4.0, array_shape, jnp.float32)


def draw_descriptors(key, part):
    center = shared_center(key)
    return (0.85 * center[None, :] + rough_noise(jax.random.fold_in(key, 21), (ATOMS, DESC))).astype(jnp.bfloat16)


def draw_gradients(key, part):
    center = shared_center(key)
    amplitude = jax.random.truncated_normal(jax.random.fold_in(key, 31), -3.0, 3.0, (3, NEIGH, ATOMS, 1), jnp.float32)
    return (0.35 * amplitude * center + 0.2 * rough_noise(jax.random.fold_in(key, 32), (3, NEIGH, ATOMS, DESC))).astype(jnp.bfloat16)


def draw_sparse_panel(key, part):
    center = shared_center(key)
    return ((0.85 * center[None, :] + rough_noise(jax.random.fold_in(key, 41), (PANEL, DESC))) * DESC ** (-0.5)).astype(jnp.bfloat16)


def draw_sparse_trail(key, part):
    center = shared_center(key)
    return ((0.85 * center[None, :] + rough_noise(jax.random.fold_in(key, 51), (TRAIL, DESC))) * DESC ** (-0.5)).astype(jnp.bfloat16)


def place_ends(drawn, key, least, largest):
    dims = drawn.shape
    place = [jax.random.randint(jax.random.fold_in(key, axis), (), 0, dims[axis]) for axis in range(len(dims))]
    drawn = drawn.at[tuple(place)].set(least)
    longest = dims.index(max(dims))
    place[longest] = (place[longest] + 1) % dims[longest]
    return drawn.at[tuple(place)].set(largest)


def split_up(number_of, total, reach, slope):
    loads = [(1 << 20) // math.isqrt(rank ** slope) + 1 for rank in range(2, number_of + 1)]
    rest, counts = total - reach - (number_of - 1), [1] * (number_of - 1)
    while rest > 0:
        free = [i for i in range(number_of - 1) if counts[i] < reach]
        whole, remaining = sum([loads[i] for i in free]), rest
        for i in free:
            extra = min(reach - counts[i], max(1, remaining * loads[i] // whole), rest)
            counts[i] = counts[i] + extra
            rest = rest - extra
    return np.array([reach] + counts)


def ragged_sizes(rng, count, total, reach, slope):
    if count == 2:
        one = jax.random.randint(rng, (), max(1, total - reach), min(reach, total - 1) + 1)
        return jnp.stack([one, total - one])
    lengths = jnp.asarray(split_up(count, total, reach, slope), jnp.int32)
    couples = (count - 1) // 2
    giver, taker = lengths[1:1 + 2 * couples:2], lengths[2:2 + 2 * couples:2]
    slack = jnp.minimum(giver - 1, reach - taker)
    passed = jax.random.randint(jax.random.fold_in(rng, 1), (couples,), 0, 1 << 20) % (slack + 1)
    lengths = lengths.at[1:1 + 2 * couples:2].set(giver - passed).at[2:2 + 2 * couples:2].set(taker + passed)
    return lengths[jax.random.permutation(jax.random.fold_in(rng, 2), count)]


def setup_inputs(seed: int = 0) -> dict:
    keys = jax.random.split(jax.random.key(seed), 8)
    descriptors = draw_descriptors(jax.random.fold_in(keys[7], 71), 0)
    gradients = draw_gradients(jax.random.fold_in(keys[7], 71), 0)
    sparse_panel = draw_sparse_panel(jax.random.fold_in(keys[7], 71), 0)
    sparse_trail = draw_sparse_trail(jax.random.fold_in(keys[7], 71), 0)
    atom_counts = jax.vmap(lambda own: ragged_sizes(own, STRUCT_DEV, ATOM_DEV, AMAX, 1))(jax.random.split(keys[4], DEVICES)).reshape((DEVICES, STRUCT_DEV)).astype(jnp.int32)
    owner_rows = jax.vmap(lambda own: jax.random.permutation(own, N_ROW))(jax.random.split(keys[5], DEVICES)).reshape((DEVICES, STRUCT_DEV)).astype(jnp.int32)
    neighbor_ids = place_ends(jax.random.randint(keys[6], (STRUCTS, AMAX, NEIGH), 0, 65520), jax.random.fold_in(keys[6], 1), 0, 65519).astype(jnp.int32)
    return dict(descriptors=descriptors, gradients=gradients, sparse_panel=sparse_panel, sparse_trail=sparse_trail, atom_counts=atom_counts, owner_rows=owner_rows, neighbor_ids=neighbor_ids)


ridge_value = 0.1

def slot_rows(environments, desc_here, slope_here, count_here, neighbor_here, owner_here):
    struct_count = count_here.shape[0]
    atom_slots = neighbor_here.shape[1]
    neighbor_count = neighbor_here.shape[2]
    env_count = environments.shape[0]
    correlation = lax.dot_general(environments.astype(jnp.float32), desc_here.astype(jnp.float32), (((1,), (1,)), ((), ())), preferred_element_type=jnp.float32)
    slope_dots = lax.dot_general(environments.astype(jnp.float32), slope_here.astype(jnp.float32), (((1,), (1,)), ((), ())), preferred_element_type=jnp.float32)
    slope_dots = slope_dots.reshape(env_count, 3, neighbor_count, struct_count, atom_slots)
    slot_index = jnp.arange(atom_slots, dtype=jnp.int32)
    live_mask = (slot_index[None, :] < count_here[:, None]).astype(jnp.float32)
    squares = (correlation * correlation).reshape(env_count, struct_count, atom_slots)
    energy = jnp.sum(squares * live_mask[None], axis=2) / count_here.astype(jnp.float32)[None, :]
    partner = neighbor_here % count_here[:, None, None]
    struct_index = jnp.arange(struct_count, dtype=jnp.int32)
    flat_index = (struct_index[:, None, None] * atom_slots + partner).reshape(-1).astype(jnp.int32)
    picked = jnp.take(correlation, flat_index, axis=1).reshape(env_count, struct_count, atom_slots, neighbor_count)
    picked = jnp.transpose(picked, (0, 3, 1, 2))
    forces = -2.0 * jnp.sum(picked[:, None] * slope_dots, axis=2) * live_mask[None, None]
    forces = jnp.transpose(forces, (0, 2, 3, 1)).reshape(env_count, struct_count, 3 * atom_slots)
    padding = jnp.zeros((env_count, struct_count, atom_slots - 1), jnp.float32)
    slot_values = jnp.concatenate([energy[:, :, None], forces, padding], axis=2).astype(jnp.bfloat16)
    chosen = (owner_here[None, :] == struct_index[:, None]).astype(jnp.int32)
    owner_order = jnp.sum(struct_index[None, :] * chosen, axis=1).astype(jnp.int32)
    return jnp.take(slot_values, owner_order, axis=1)

def factor_panel(gram_sum, cross_sum, total_rows):
    gram_matrix = gram_sum / total_rows + ridge_value * jnp.eye(gram_sum.shape[0], dtype=jnp.float32)
    lower_factor = jnp.linalg.cholesky(gram_matrix)
    coupling = lax.linalg.triangular_solve(lower_factor, cross_sum / total_rows, left_side=True, lower=True)
    weights = lax.linalg.triangular_solve(lower_factor, coupling, left_side=True, lower=True, transpose_a=True)
    return (lower_factor.T, coupling, weights)

def split_weights(weights):
    weight_high = weights.astype(jnp.bfloat16)
    held_high = lax.optimization_barrier(weight_high)
    weight_low = (weights - held_high.astype(jnp.float32)).astype(jnp.bfloat16)
    return (weight_high, weight_low)

def reference(descriptors, gradients, sparse_panel, sparse_trail, atom_counts, owner_rows, neighbor_ids):
    environments = jnp.concatenate([sparse_panel, sparse_trail], axis=0)
    env_count = environments.shape[0]
    atoms_dev = N_ROW * AMAX

    def one_device(device_index):
        desc_here = lax.dynamic_slice_in_dim(descriptors, device_index * atoms_dev, atoms_dev, 0)
        slope_here = lax.dynamic_slice_in_dim(gradients, device_index * atoms_dev, atoms_dev, 2).reshape(-1, DESC)
        count_here = lax.dynamic_index_in_dim(atom_counts, device_index, 0, keepdims=False)
        owner_here = lax.dynamic_index_in_dim(owner_rows, device_index, 0, keepdims=False)
        neighbor_here = lax.dynamic_slice_in_dim(neighbor_ids, device_index * N_ROW, N_ROW, 0)
        return slot_rows(environments, desc_here, slope_here, count_here, neighbor_here, owner_here)
    per_device = lax.map(one_device, jnp.arange(DEVICES, dtype=jnp.int32))
    slot_count = per_device.shape[3]
    design = jnp.transpose(per_device.reshape(N_ROW, N_COL, env_count, N_ROW, slot_count), (2, 3, 1, 0, 4)).reshape(env_count, ROWS)
    design_panel = design[:PANEL]
    design_trail = design[PANEL:]
    gram_sum = lax.dot_general(design_panel.astype(jnp.float32), design_panel.astype(jnp.float32), (((1,), (1,)), ((), ())), preferred_element_type=jnp.float32)
    cross_sum = lax.dot_general(design_panel.astype(jnp.float32), design_trail.astype(jnp.float32), (((1,), (1,)), ((), ())), preferred_element_type=jnp.float32)
    panel_factor, coupling, weights = factor_panel(gram_sum, cross_sum, ROWS)
    weight_high, weight_low = split_weights(weights)
    projected = lax.dot_general(weight_high.astype(jnp.float32), design_panel.astype(jnp.float32), (((0,), (0,)), ((), ())), preferred_element_type=jnp.float32)
    projected = projected + lax.dot_general(weight_low.astype(jnp.float32), design_panel.astype(jnp.float32), (((0,), (0,)), ((), ())), preferred_element_type=jnp.float32)
    trail_residual = design_trail.astype(jnp.float32) - projected
    return (panel_factor, coupling.T, trail_residual)
```

```python
import jax
import jax.numpy as jnp
from jax import lax
from jax.experimental import pallas as pl
from jax.experimental.pallas import tpu as pltpu
from jax.sharding import PartitionSpec as P

ridge_value = 0.1


def slot_rows(environments, desc_here, slope_here, count_here, neighbor_here, owner_here):
    struct_count = count_here.shape[0]
    atom_slots = neighbor_here.shape[1]
    neighbor_count = neighbor_here.shape[2]
    env_count = environments.shape[0]
    correlation = lax.dot_general(
        environments, desc_here, (((1,), (1,)), ((), ())), preferred_element_type=jnp.float32
    )
    slope_dots = lax.dot_general(
        environments, slope_here, (((1,), (1,)), ((), ())), preferred_element_type=jnp.float32
    )
    slope_dots = slope_dots.reshape(env_count, 3, neighbor_count, struct_count, atom_slots)
    slot_index = jnp.arange(atom_slots, dtype=jnp.int32)
    live_mask = (slot_index[None, :] < count_here[:, None]).astype(jnp.float32)
    squares = (correlation * correlation).reshape(env_count, struct_count, atom_slots)
    energy = jnp.sum(squares * live_mask[None], axis=2) / count_here.astype(jnp.float32)[None, :]
    partner = neighbor_here % count_here[:, None, None]
    struct_index = jnp.arange(struct_count, dtype=jnp.int32)
    flat_index = (struct_index[:, None, None] * atom_slots + partner).reshape(-1)
    picked = jnp.take(correlation, flat_index, axis=1).reshape(
        env_count, struct_count, atom_slots, neighbor_count
    )
    picked = jnp.transpose(picked, (0, 3, 1, 2))
    forces = -2.0 * jnp.sum(picked[:, None] * slope_dots, axis=2) * live_mask[None, None]
    forces = jnp.transpose(forces, (0, 2, 3, 1)).reshape(env_count, struct_count, 3 * atom_slots)
    padding = jnp.zeros((env_count, struct_count, atom_slots - 1), jnp.float32)
    slot_values = jnp.concatenate([energy[:, :, None], forces, padding], axis=2).astype(
        jnp.bfloat16
    )
    chosen = (owner_here[None, :] == struct_index[:, None]).astype(jnp.int32)
    owner_order = jnp.sum(struct_index[None, :] * chosen, axis=1)
    return jnp.take(slot_values, owner_order, axis=1)


GROUP = 8
BLOCK = 128


def exact_dot(left_side, right_side, left_dim, right_dim):
    return lax.dot_general(
        left_side,
        right_side,
        (((left_dim,), (right_dim,)), ((), ())),
        preferred_element_type=jnp.float32,
        precision=lax.Precision.HIGHEST,
    )


def spread_row(values, row):
    return jnp.broadcast_to(values[row : row + 1, :], values.shape)


def eliminate_group(work_ref, group):
    first = pl.multiple_of(group * GROUP, GROUP)
    rows = work_ref[pl.ds(first, GROUP), :]
    diag = rows[:, :BLOCK]
    lanes = lax.broadcasted_iota(jnp.int32, (GROUP, BLOCK), 1)
    sub = lax.broadcasted_iota(jnp.int32, (GROUP, BLOCK), 0)
    sub_wide = lax.broadcasted_iota(jnp.int32, (GROUP, 2 * BLOCK), 0)
    columns = [
        jnp.broadcast_to(
            jnp.sum(jnp.where(lanes == first + j, diag, 0.0), axis=1, keepdims=True),
            (GROUP, BLOCK),
        )
        for j in range(GROUP)
    ]
    for j in range(GROUP):
        pivot = spread_row(columns[j], j)
        inverse = lax.rsqrt(pivot)
        inverse = inverse * (1.5 - 0.5 * pivot * inverse * inverse)
        scale = jnp.where(sub > j, columns[j] * inverse, 0.0)
        for m in range(j + 1, GROUP):
            columns[m] = columns[m] - scale * (spread_row(columns[m], j) * inverse)
        both = jnp.concatenate([inverse, inverse], axis=1)
        scale_both = jnp.concatenate([scale, scale], axis=1)
        scaled = spread_row(rows, j) * both
        rows = jnp.where(sub_wide == j, scaled, rows - scale_both * scaled)
    work_ref[pl.ds(first, GROUP), :] = rows
    later = jnp.where(lanes >= first + GROUP, rows[:, :BLOCK], 0.0)
    work_ref[...] -= exact_dot(later, rows, 0, 0)


def factor_kernel(
    total_rows,
    gram_ref,
    cross_ref,
    factor_ref,
    coupled_ref,
    high_ref,
    low_ref,
    field_ref,
    work_ref,
    inverse_ref,
    weight_ref,
):
    size = gram_ref.shape[0]
    blocks = size // BLOCK
    row_ids = lax.broadcasted_iota(jnp.int32, (BLOCK, BLOCK), 0)
    col_ids = lax.broadcasted_iota(jnp.int32, (BLOCK, BLOCK), 1)
    unit = (row_ids == col_ids).astype(jnp.float32)
    field_ref[:, :size] = gram_ref[...] / total_rows
    field_ref[:, size:] = cross_ref[...] / total_rows
    factor_ref[...] = jnp.zeros_like(factor_ref)
    for b in range(blocks):
        here = slice(b * BLOCK, (b + 1) * BLOCK)
        after = (b + 1) * BLOCK
        work_ref[:, :BLOCK] = field_ref[here, here] + ridge_value * unit
        work_ref[:, BLOCK:] = unit

        def step(group, carry):
            eliminate_group(work_ref, group)
            return carry

        lax.fori_loop(0, BLOCK // GROUP, step, 0)
        factor_ref[here, here] = jnp.where(col_ids >= row_ids, work_ref[:, :BLOCK], 0.0)
        inverse = work_ref[:, BLOCK:]
        inverse_ref[here, :] = inverse
        row_rest = exact_dot(inverse, field_ref[here, after:], 1, 0)
        field_ref[here, after:] = row_rest
        if after < size:
            factor_ref[here, after:] = row_rest[:, : size - after]
            field_ref[after:, after:] -= exact_dot(row_rest[:, : size - after], row_rest, 0, 0)
        coupled_ref[:, here] = row_rest[:, size - after :].T
    for b in range(blocks - 1, -1, -1):
        here = slice(b * BLOCK, (b + 1) * BLOCK)
        after = (b + 1) * BLOCK
        rest = field_ref[here, size:]
        if after < size:
            rest = rest - exact_dot(factor_ref[here, after:], weight_ref[after:, :], 1, 0)
        weight_ref[here, :] = exact_dot(inverse_ref[here, :], rest, 0, 0)
    weights = weight_ref[...]
    high = weights.astype(jnp.bfloat16)
    high_ref[...] = high
    low_ref[...] = (weights - high.astype(jnp.float32)).astype(jnp.bfloat16)


def factor_panel(gram_sum, cross_sum, total_rows):
    size, width = cross_sum.shape
    return pl.pallas_call(
        lambda *refs: factor_kernel(total_rows, *refs),
        out_shape=(
            jax.ShapeDtypeStruct((size, size), jnp.float32),
            jax.ShapeDtypeStruct((width, size), jnp.float32),
            jax.ShapeDtypeStruct((size, width), jnp.bfloat16),
            jax.ShapeDtypeStruct((size, width), jnp.bfloat16),
        ),
        scratch_shapes=[
            pltpu.VMEM((size, size + width), jnp.float32),
            pltpu.VMEM((BLOCK, 2 * BLOCK), jnp.float32),
            pltpu.VMEM((size, BLOCK), jnp.float32),
            pltpu.VMEM((size, width), jnp.float32),
        ],
        compiler_params=pltpu.CompilerParams(vmem_limit_bytes=32 * 1024 * 1024),
        name="factor_panel",
    )(gram_sum, cross_sum)


def contract_rows(left_side, right_side):
    return lax.dot_general(
        left_side, right_side, (((1,), (1,)), ((), ())), preferred_element_type=jnp.float32
    )


def contract_cols(left_side, right_side):
    return lax.dot_general(
        left_side, right_side, (((0,), (0,)), ((), ())), preferred_element_type=jnp.float32
    )


def arrange_direct(block_rows, row_count, col_count):
    env_width = block_rows.shape[0] // col_count
    slot_count = block_rows.shape[2]
    shaped = block_rows.reshape(col_count, env_width, row_count, slot_count)
    return jnp.transpose(shaped, (2, 0, 1, 3)).reshape(row_count * col_count, env_width, slot_count)


def restore_direct(block_rows, row_count, col_count):
    env_width = block_rows.shape[1]
    slot_count = block_rows.shape[2]
    shaped = block_rows.reshape(row_count, col_count, env_width, slot_count)
    return jnp.transpose(shaped, (2, 1, 0, 3)).reshape(
        env_width, row_count * col_count * slot_count
    )


def per_device(
    descriptors, gradients, sparse_panel, sparse_trail, atom_counts, owner_rows, neighbor_ids
):
    row_count = lax.axis_size("row")
    col_count = lax.axis_size("col")
    count_here = atom_counts[0]
    owner_here = owner_rows[0]
    slope_here = gradients.reshape(-1, gradients.shape[3])
    panel_width = sparse_panel.shape[0]
    trail_width = sparse_trail.shape[0]
    panel_total = panel_width * col_count
    trail_total = trail_width * col_count
    slot_count = 4 * neighbor_ids.shape[1]
    total_rows = row_count * row_count * col_count * slot_count
    own_envs = jnp.concatenate([sparse_panel, sparse_trail], axis=0)
    kernel_rows = slot_rows(
        lax.all_gather(own_envs, "col", axis=0, tiled=True),
        descriptors,
        slope_here,
        count_here,
        neighbor_ids,
        owner_here,
    )
    blocks = kernel_rows.reshape(col_count, panel_width + trail_width, row_count, slot_count)
    panel_rows = blocks[:, :panel_width].reshape(panel_total, row_count, slot_count)
    trail_rows = blocks[:, panel_width:].reshape(trail_total, row_count, slot_count)
    received = (
        lax.all_to_all(
            arrange_direct(panel_rows, row_count, col_count),
            ("row", "col"),
            split_axis=0,
            concat_axis=0,
            tiled=True,
        ),
        lax.all_to_all(
            arrange_direct(trail_rows, row_count, col_count),
            ("row", "col"),
            split_axis=0,
            concat_axis=0,
            tiled=True,
        ),
    )
    panel_own = restore_direct(received[0], row_count, col_count)
    trail_own = restore_direct(received[1], row_count, col_count)
    segment = lax.all_gather(panel_own, "col", axis=0, tiled=True)
    own_rows = jnp.concatenate([panel_own, trail_own], axis=0)
    products = lax.psum(contract_rows(own_rows, segment), "row")
    gram_sum = lax.all_gather(products[:panel_width], "col", axis=0, tiled=True)
    cross_sum = products[panel_width:].T
    panel_factor, cross_factor, weight_high, weight_low = factor_panel(
        gram_sum, cross_sum, total_rows
    )
    trail_residual = (
        trail_own.astype(jnp.float32)
        - contract_cols(weight_high, segment)
        - contract_cols(weight_low, segment)
    )
    return (panel_factor, cross_factor, trail_residual)


def solution(mesh):
    return jax.shard_map(
        per_device,
        mesh=mesh,
        in_specs=(
            P(("row", "col"), None),
            P(None, None, ("row", "col"), None),
            P("col", None),
            P("col", None),
            P(("row", "col"), None),
            P(("row", "col"), None),
            P(("row", "col"), None, None),
        ),
        out_specs=(P(), P("col", None), P("col", "row")),
        check_vma=False,
    )
```

```python
import jax
import jax.numpy as jnp
from jax import lax
from jax.experimental import pallas as pl
from jax.experimental.pallas import tpu as pltpu
from jax.sharding import PartitionSpec as P

ridge_value = 0.1


def slot_rows(environments, desc_here, slope_here, count_here, neighbor_here, owner_here):
    struct_count = count_here.shape[0]
    atom_slots = neighbor_here.shape[1]
    neighbor_count = neighbor_here.shape[2]
    env_count = environments.shape[0]
    correlation = lax.dot_general(
        environments, desc_here, (((1,), (1,)), ((), ())), preferred_element_type=jnp.float32
    )
    slope_dots = lax.dot_general(
        environments, slope_here, (((1,), (1,)), ((), ())), preferred_element_type=jnp.float32
    )
    slope_dots = slope_dots.reshape(env_count, 3, neighbor_count, struct_count, atom_slots)
    slot_index = jnp.arange(atom_slots, dtype=jnp.int32)
    live_mask = (slot_index[None, :] < count_here[:, None]).astype(jnp.float32)
    squares = (correlation * correlation).reshape(env_count, struct_count, atom_slots)
    energy = jnp.sum(squares * live_mask[None], axis=2) / count_here.astype(jnp.float32)[None, :]
    partner = neighbor_here % count_here[:, None, None]
    struct_index = jnp.arange(struct_count, dtype=jnp.int32)
    flat_index = (struct_index[:, None, None] * atom_slots + partner).reshape(-1)
    picked = jnp.take(correlation, flat_index, axis=1).reshape(
        env_count, struct_count, atom_slots, neighbor_count
    )
    picked = jnp.transpose(picked, (0, 3, 1, 2))
    forces = -2.0 * jnp.sum(picked[:, None] * slope_dots, axis=2) * live_mask[None, None]
    forces = jnp.transpose(forces, (0, 2, 3, 1)).reshape(env_count, struct_count, 3 * atom_slots)
    padding = jnp.zeros((env_count, struct_count, atom_slots - 1), jnp.float32)
    slot_values = jnp.concatenate([energy[:, :, None], forces, padding], axis=2).astype(
        jnp.bfloat16
    )
    chosen = (owner_here[None, :] == struct_index[:, None]).astype(jnp.int32)
    owner_order = jnp.sum(struct_index[None, :] * chosen, axis=1)
    return jnp.take(slot_values, owner_order, axis=1)


GROUP = 8
BLOCK = 128


def exact_dot(left_side, right_side, left_dim, right_dim):
    return lax.dot_general(
        left_side,
        right_side,
        (((left_dim,), (right_dim,)), ((), ())),
        preferred_element_type=jnp.float32,
        precision=lax.Precision.HIGHEST,
    )


def spread_row(values, row):
    return jnp.broadcast_to(values[row : row + 1, :], values.shape)


def eliminate_group(work_ref, group):
    first = pl.multiple_of(group * GROUP, GROUP)
    rows = work_ref[pl.ds(first, GROUP), :]
    diag = rows[:, :BLOCK]
    lanes = lax.broadcasted_iota(jnp.int32, (GROUP, BLOCK), 1)
    sub = lax.broadcasted_iota(jnp.int32, (GROUP, BLOCK), 0)
    sub_wide = lax.broadcasted_iota(jnp.int32, (GROUP, 2 * BLOCK), 0)
    columns = [
        jnp.broadcast_to(
            jnp.sum(jnp.where(lanes == first + j, diag, 0.0), axis=1, keepdims=True),
            (GROUP, BLOCK),
        )
        for j in range(GROUP)
    ]
    for j in range(GROUP):
        pivot = spread_row(columns[j], j)
        inverse = lax.rsqrt(pivot)
        inverse = inverse * (1.5 - 0.5 * pivot * inverse * inverse)
        scale = jnp.where(sub > j, columns[j] * inverse, 0.0)
        for m in range(j + 1, GROUP):
            columns[m] = columns[m] - scale * (spread_row(columns[m], j) * inverse)
        both = jnp.concatenate([inverse, inverse], axis=1)
        scale_both = jnp.concatenate([scale, scale], axis=1)
        scaled = spread_row(rows, j) * both
        rows = jnp.where(sub_wide == j, scaled, rows - scale_both * scaled)
    work_ref[pl.ds(first, GROUP), :] = rows
    later = jnp.where(lanes >= first + GROUP, rows[:, :BLOCK], 0.0)
    work_ref[...] -= exact_dot(later, rows, 0, 0)


def factor_kernel(
    total_rows,
    gram_ref,
    cross_ref,
    factor_ref,
    coupled_ref,
    high_ref,
    low_ref,
    field_ref,
    work_ref,
    inverse_ref,
    weight_ref,
):
    size = gram_ref.shape[0]
    blocks = size // BLOCK
    row_ids = lax.broadcasted_iota(jnp.int32, (BLOCK, BLOCK), 0)
    col_ids = lax.broadcasted_iota(jnp.int32, (BLOCK, BLOCK), 1)
    unit = (row_ids == col_ids).astype(jnp.float32)
    field_ref[:, :size] = gram_ref[...] / total_rows
    field_ref[:, size:] = cross_ref[...] / total_rows
    factor_ref[...] = jnp.zeros_like(factor_ref)
    for b in range(blocks):
        here = slice(b * BLOCK, (b + 1) * BLOCK)
        after = (b + 1) * BLOCK
        work_ref[:, :BLOCK] = field_ref[here, here] + ridge_value * unit
        work_ref[:, BLOCK:] = unit

        def step(group, carry):
            eliminate_group(work_ref, group)
            return carry

        lax.fori_loop(0, BLOCK // GROUP, step, 0)
        factor_ref[here, here] = jnp.where(col_ids >= row_ids, work_ref[:, :BLOCK], 0.0)
        inverse = work_ref[:, BLOCK:]
        inverse_ref[here, :] = inverse
        row_rest = exact_dot(inverse, field_ref[here, after:], 1, 0)
        field_ref[here, after:] = row_rest
        if after < size:
            factor_ref[here, after:] = row_rest[:, : size - after]
            field_ref[after:, after:] -= exact_dot(row_rest[:, : size - after], row_rest, 0, 0)
        coupled_ref[:, here] = row_rest[:, size - after :].T
    for b in range(blocks - 1, -1, -1):
        here = slice(b * BLOCK, (b + 1) * BLOCK)
        after = (b + 1) * BLOCK
        rest = field_ref[here, size:]
        if after < size:
            rest = rest - exact_dot(factor_ref[here, after:], weight_ref[after:, :], 1, 0)
        weight_ref[here, :] = exact_dot(inverse_ref[here, :], rest, 0, 0)
    weights = weight_ref[...]
    high = weights.astype(jnp.bfloat16)
    high_ref[...] = high
    low_ref[...] = (weights - high.astype(jnp.float32)).astype(jnp.bfloat16)


def factor_panel(gram_sum, cross_sum, total_rows):
    size, width = cross_sum.shape
    return pl.pallas_call(
        lambda *refs: factor_kernel(total_rows, *refs),
        out_shape=(
            jax.ShapeDtypeStruct((size, size), jnp.float32),
            jax.ShapeDtypeStruct((width, size), jnp.float32),
            jax.ShapeDtypeStruct((size, width), jnp.bfloat16),
            jax.ShapeDtypeStruct((size, width), jnp.bfloat16),
        ),
        scratch_shapes=[
            pltpu.VMEM((size, size + width), jnp.float32),
            pltpu.VMEM((BLOCK, 2 * BLOCK), jnp.float32),
            pltpu.VMEM((size, BLOCK), jnp.float32),
            pltpu.VMEM((size, width), jnp.float32),
        ],
        compiler_params=pltpu.CompilerParams(vmem_limit_bytes=32 * 1024 * 1024),
        name="factor_panel",
    )(gram_sum, cross_sum)


MESH = pl.DeviceIdType.MESH
VMEM_SPEC = pl.BlockSpec(memory_space=pltpu.VMEM)


def split_axis(count):
    inner = 1
    while 4 * inner * inner <= count:
        inner *= 2
    return count // inner, inner


def here_and_peers(row_count, col_count):
    row, col = lax.axis_index("row"), lax.axis_index("col")
    outer, inner = split_axis(col_count)
    core, lane = row % 2, col % inner
    sibling = row + 1 - 2 * core
    far = [(row, ((col // inner + d) % outer) * inner + lane) for d in range(1, outer)]
    near = [(row, (col // inner) * inner + (lane + e) % inner) for e in range(1, inner)]
    level = [((row + 2 * d) % row_count, col) for d in range(1, row_count // 2)]
    return row, col, core, (sibling, col), far, near, level


def greet(peers):
    barrier = pltpu.get_barrier_semaphore()
    for peer in peers:
        pl.semaphore_signal(barrier, inc=1, device_id=peer, device_id_type=MESH)
    pl.semaphore_wait(barrier, len(peers))


def remote(source, target, send_sem, recv_sem, peer):
    return pltpu.make_async_remote_copy(
        src_ref=source,
        dst_ref=target,
        send_sem=send_sem,
        recv_sem=recv_sem,
        device_id=peer,
        device_id_type=MESH,
    )


def relay(parts, count, place, far_sem, near_sem, side_sem, recv_sem):
    row, col, core, sibling, far, near, _ = place
    started = []

    def send(part, block, sem, peer):
        ref = parts(core, block)[part]
        copy = remote(ref, ref, sem, recv_sem.at[part, core, block], peer)
        copy.start()
        started.append(copy)

    def arrived(part, which, block):
        ref = parts(which, block)[part]
        remote(ref, ref, side_sem.at[part, 0], recv_sem.at[part, which, block], sibling).wait_recv()

    def pass_on(part, block, step):
        for e, peer in enumerate(near):
            send(part, block, near_sem.at[part, step, e], peer)
        send(part, block, side_sem.at[part, step], sibling)

    for part in range(count):
        for d, peer in enumerate(far):
            send(part, col, far_sem.at[part, d], peer)
    for part in range(count):
        pass_on(part, col, 0)
    outer, inner = len(far) + 1, len(near) + 1
    for d in range(1, outer):
        block = far[d - 1][1]
        for part in range(count):
            arrived(part, core, block)
            pass_on(part, block, d)
    home, lane = col // inner, col % inner
    for d in range(outer):
        for e in range(1, inner):
            block = ((home + d) % outer) * inner + (lane + e) % inner
            for part in range(count):
                arrived(part, core, block)
                send(part, block, side_sem.at[part, e * outer + d], sibling)
    for block in range(outer * inner):
        for part in range(count):
            arrived(part, 1 - core, block)
    for copy in started:
        copy.wait_send()


def relay_sems(count, col_count):
    outer, inner = split_axis(col_count)
    return [
        pltpu.SemaphoreType.DMA((count, outer)),
        pltpu.SemaphoreType.DMA((count, outer, inner)),
        pltpu.SemaphoreType.DMA((count, col_count)),
        pltpu.SemaphoreType.DMA((count, 2, col_count)),
    ]


def gather_kernel(
    row_count, col_count, panel_ref, trail_ref, panels_ref, trails_ref, own_sem, *sems
):
    place = here_and_peers(row_count, col_count)
    row, col, core, sibling, far, near, _ = place
    panel_width, trail_width = panel_ref.shape[0], trail_ref.shape[0]
    half = panel_ref.shape[1] // 2

    def lanes(which):
        return pl.ds(pl.multiple_of(which * half, half), half)

    def parts(which, block):
        panel_rows = pl.ds(pl.multiple_of(block * panel_width, panel_width), panel_width)
        trail_rows = pl.ds(pl.multiple_of(block * trail_width, trail_width), trail_width)
        return [panels_ref.at[panel_rows, lanes(which)], trails_ref.at[trail_rows, lanes(which)]]

    own = parts(core, col)
    copies = [
        pltpu.make_async_copy(panel_ref.at[:, lanes(core)], own[0], own_sem.at[0]),
        pltpu.make_async_copy(trail_ref.at[:, lanes(core)], own[1], own_sem.at[1]),
    ]
    for copy in copies:
        copy.start()
    greet([sibling, *far, *near])
    for copy in copies:
        copy.wait()
    relay(parts, 2, place, *sems)


def gather_environments(sparse_panel, sparse_trail, row_count, col_count):
    depth = sparse_panel.shape[1]
    return pl.pallas_call(
        lambda *refs: gather_kernel(row_count, col_count, *refs),
        out_shape=(
            jax.ShapeDtypeStruct((col_count * sparse_panel.shape[0], depth), sparse_panel.dtype),
            jax.ShapeDtypeStruct((col_count * sparse_trail.shape[0], depth), sparse_trail.dtype),
        ),
        in_specs=[VMEM_SPEC] * 2,
        out_specs=(VMEM_SPEC, VMEM_SPEC),
        scratch_shapes=[pltpu.SemaphoreType.DMA((2,)), *relay_sems(2, col_count)],
        compiler_params=pltpu.CompilerParams(
            collective_id=1, has_side_effects=True, vmem_limit_bytes=32 * 1024 * 1024
        ),
        name="gather_environments",
    )(sparse_panel, sparse_trail)


def sum_kernel(
    row_count,
    col_count,
    gram_part,
    cross_part,
    gram_ref,
    cross_ref,
    side_ref,
    level_ref,
    side_send,
    side_recv,
    level_send,
    level_recv,
    cross_send,
    cross_recv,
    *sems,
):
    place = here_and_peers(row_count, col_count)
    row, col, core, sibling, far, near, level = place
    gram_half = gram_part.shape[0] // 2
    cross_half = cross_part.shape[0] // 2
    greet([sibling, *far, *near, *level])

    def gram_rows(which):
        return pl.ds(pl.multiple_of(which * gram_half, gram_half), gram_half)

    def cross_rows(which):
        return pl.ds(pl.multiple_of(which * cross_half, cross_half), cross_half)

    to_side = [
        remote(
            gram_part.at[gram_rows(1 - core)],
            side_ref.at[:gram_half],
            side_send.at[0],
            side_recv.at[0],
            sibling,
        ),
        remote(
            cross_part.at[cross_rows(1 - core)],
            side_ref.at[gram_half:],
            side_send.at[1],
            side_recv.at[1],
            sibling,
        ),
    ]
    for copy in to_side:
        copy.start()
    for copy in to_side:
        copy.wait()
    floor = row // 2
    level_ref[floor, :gram_half] = gram_part[gram_rows(core), :] + side_ref[:gram_half]
    level_ref[floor, gram_half:] = cross_part[cross_rows(core), :] + side_ref[gram_half:]
    to_level = []
    for d, peer in enumerate(level):
        mine = level_ref.at[floor]
        copy = remote(mine, mine, level_send.at[d], level_recv.at[floor], peer)
        copy.start()
        to_level.append(copy)
    for d, peer in enumerate(level):
        other = peer[0] // 2
        theirs = level_ref.at[other]
        remote(theirs, theirs, level_send.at[d], level_recv.at[other], peer).wait_recv()
    total = level_ref[0]
    for other in range(1, row_count // 2):
        total = total + level_ref[other]

    def parts(which, block):
        first = block * (2 * gram_half) + which * gram_half
        return [gram_ref.at[pl.ds(pl.multiple_of(first, gram_half), gram_half)]]

    parts(core, col)[0][...] = total[:gram_half]
    cross_ref[cross_rows(core), :] = total[gram_half:]
    mine = cross_ref.at[cross_rows(core)]
    to_cross = remote(mine, mine, cross_send.at[0], cross_recv.at[0], sibling)
    to_cross.start()
    relay(parts, 1, place, *sems)
    to_cross.wait()
    for copy in to_level:
        copy.wait_send()


def sum_products(gram_part, cross_part, row_count, col_count):
    width = gram_part.shape[1]
    half = (gram_part.shape[0] + cross_part.shape[0]) // 2
    levels = row_count // 2
    return pl.pallas_call(
        lambda *refs: sum_kernel(row_count, col_count, *refs),
        out_shape=(
            jax.ShapeDtypeStruct((gram_part.shape[0] * col_count, width), jnp.float32),
            jax.ShapeDtypeStruct(cross_part.shape, jnp.float32),
        ),
        in_specs=[VMEM_SPEC] * 2,
        out_specs=(VMEM_SPEC, VMEM_SPEC),
        scratch_shapes=[
            pltpu.VMEM((half, width), jnp.float32),
            pltpu.VMEM((levels, half, width), jnp.float32),
            pltpu.SemaphoreType.DMA((2,)),
            pltpu.SemaphoreType.DMA((2,)),
            pltpu.SemaphoreType.DMA((levels,)),
            pltpu.SemaphoreType.DMA((levels,)),
            pltpu.SemaphoreType.DMA((1,)),
            pltpu.SemaphoreType.DMA((1,)),
            *relay_sems(1, col_count),
        ],
        compiler_params=pltpu.CompilerParams(
            collective_id=2, has_side_effects=True, vmem_limit_bytes=32 * 1024 * 1024
        ),
        name="sum_products",
    )(gram_part, cross_part)


def contract_rows(left_side, right_side):
    return lax.dot_general(
        left_side, right_side, (((1,), (1,)), ((), ())), preferred_element_type=jnp.float32
    )


def contract_cols(left_side, right_side):
    return lax.dot_general(
        left_side, right_side, (((0,), (0,)), ((), ())), preferred_element_type=jnp.float32
    )


def arrange_direct(block_rows, row_count, col_count):
    env_width = block_rows.shape[0] // col_count
    slot_count = block_rows.shape[2]
    shaped = block_rows.reshape(col_count, env_width, row_count, slot_count)
    return jnp.transpose(shaped, (2, 0, 1, 3)).reshape(row_count * col_count, env_width, slot_count)


def restore_direct(block_rows, row_count, col_count):
    env_width = block_rows.shape[1]
    slot_count = block_rows.shape[2]
    shaped = block_rows.reshape(row_count, col_count, env_width, slot_count)
    return jnp.transpose(shaped, (2, 1, 0, 3)).reshape(
        env_width, row_count * col_count * slot_count
    )


def per_device(
    descriptors, gradients, sparse_panel, sparse_trail, atom_counts, owner_rows, neighbor_ids
):
    row_count = lax.axis_size("row")
    col_count = lax.axis_size("col")
    count_here = atom_counts[0]
    owner_here = owner_rows[0]
    slope_here = gradients.reshape(-1, gradients.shape[3])
    panel_width = sparse_panel.shape[0]
    trail_width = sparse_trail.shape[0]
    panel_total = panel_width * col_count
    slot_count = 4 * neighbor_ids.shape[1]
    total_rows = row_count * row_count * col_count * slot_count
    environments = jnp.concatenate(
        gather_environments(sparse_panel, sparse_trail, row_count, col_count), axis=0
    )
    kernel_rows = slot_rows(
        environments, descriptors, slope_here, count_here, neighbor_ids, owner_here
    )
    panel_rows = kernel_rows[:panel_total]
    trail_rows = kernel_rows[panel_total:]
    received = (
        lax.all_to_all(
            arrange_direct(panel_rows, row_count, col_count),
            ("row", "col"),
            split_axis=0,
            concat_axis=0,
            tiled=True,
        ),
        lax.all_to_all(
            arrange_direct(trail_rows, row_count, col_count),
            ("row", "col"),
            split_axis=0,
            concat_axis=0,
            tiled=True,
        ),
    )
    panel_own = restore_direct(received[0], row_count, col_count)
    trail_own = restore_direct(received[1], row_count, col_count)
    segment = lax.all_gather(panel_own, "col", axis=0, tiled=True)
    gram_sum, cross_sum = sum_products(
        contract_rows(panel_own, segment), contract_rows(trail_own, segment), row_count, col_count
    )
    cross_sum = cross_sum.T
    panel_factor, cross_factor, weight_high, weight_low = factor_panel(
        gram_sum, cross_sum, total_rows
    )
    trail_residual = (
        trail_own.astype(jnp.float32)
        - contract_cols(weight_high, segment)
        - contract_cols(weight_low, segment)
    )
    return (panel_factor, cross_factor, trail_residual)


def solution(mesh):
    return jax.shard_map(
        per_device,
        mesh=mesh,
        in_specs=(
            P(("row", "col"), None),
            P(None, None, ("row", "col"), None),
            P("col", None),
            P("col", None),
            P(("row", "col"), None),
            P(("row", "col"), None),
            P(("row", "col"), None, None),
        ),
        out_specs=(P(), P("col", None), P("col", "row")),
        check_vma=False,
    )
```

```python
import jax
import jax.numpy as jnp
from jax import lax
from jax.experimental import pallas as pl
from jax.experimental.pallas import tpu as pltpu
from jax.sharding import PartitionSpec as P

ridge_value = 0.1


def exact_dot(left_side, right_side, left_dim, right_dim):
    return lax.dot_general(
        left_side,
        right_side,
        (((left_dim,), (right_dim,)), ((), ())),
        preferred_element_type=jnp.float32,
        precision=lax.Precision.HIGHEST,
    )


def slot_rows(environments, desc_here, slope_here, count_here, neighbor_here, owner_here):
    struct_count, atom_slots, neighbor_count = neighbor_here.shape
    env_count = environments.shape[0]
    atoms = struct_count * atom_slots
    correlation = contract_rows(desc_here, environments)
    slope_dots = contract_rows(slope_here, environments)
    slope_dots = slope_dots.reshape(3, neighbor_count, atoms, env_count)
    slot_index = jnp.arange(atom_slots, dtype=jnp.int32)
    live_mask = (slot_index[None, :] < count_here[:, None]).astype(jnp.float32)
    squares = (correlation * correlation).reshape(struct_count, atom_slots, env_count)
    energy = jnp.sum(squares * live_mask[:, :, None], axis=1) / count_here.astype(jnp.float32)[
        :, None
    ]
    partner = neighbor_here % count_here[:, None, None]
    struct_index = jnp.arange(struct_count, dtype=jnp.int32)
    flat_index = struct_index[:, None, None] * atom_slots + partner
    flat_index = jnp.transpose(flat_index.reshape(atoms, neighbor_count))
    atom_index = jnp.arange(atoms, dtype=jnp.int32)
    chooser = jnp.where(
        flat_index[:, :, None] == atom_index, -2.0 * live_mask.reshape(1, atoms, 1), 0.0
    )
    picked = exact_dot(chooser.reshape(neighbor_count * atoms, atoms), correlation, 1, 0)
    picked = picked.reshape(1, neighbor_count, atoms, env_count)
    forces = jnp.sum(picked * slope_dots, axis=1).reshape(3 * atoms, env_count)
    values = jnp.concatenate(
        [energy.astype(jnp.bfloat16), forces.astype(jnp.bfloat16)], axis=0
    )
    chosen = (owner_here[None, :] == struct_index[:, None]).astype(jnp.int32)
    owner_order = jnp.sum(struct_index[None, :] * chosen, axis=1)[:, None]
    slot = jnp.arange(4 * atom_slots, dtype=jnp.int32)[None, :]
    atom, axis = (slot - 1) // 3, (slot - 1) % 3
    source = struct_count + axis * atoms + owner_order * atom_slots + atom
    source = jnp.where(slot <= 3 * atom_slots, source, -1)
    source = jnp.where(slot == 0, owner_order, source).reshape(-1)
    value_index = jnp.arange(values.shape[0], dtype=jnp.int32)
    placing = (source[:, None] == value_index[None, :]).astype(jnp.bfloat16)
    return lax.dot_general(
        placing, values, (((1,), (0,)), ((), ())), preferred_element_type=jnp.float32
    ).astype(jnp.bfloat16)


GROUP = 8
BLOCK = 128


def spread_row(values, row):
    return jnp.broadcast_to(values[row : row + 1, :], values.shape)


def eliminate_group(work_ref, group):
    first = pl.multiple_of(group * GROUP, GROUP)
    rows = work_ref[pl.ds(first, GROUP), :]
    diag = rows[:, :BLOCK]
    lanes = lax.broadcasted_iota(jnp.int32, (GROUP, BLOCK), 1)
    sub = lax.broadcasted_iota(jnp.int32, (GROUP, BLOCK), 0)
    sub_wide = lax.broadcasted_iota(jnp.int32, (GROUP, 2 * BLOCK), 0)
    columns = [
        jnp.broadcast_to(
            jnp.sum(jnp.where(lanes == first + j, diag, 0.0), axis=1, keepdims=True),
            (GROUP, BLOCK),
        )
        for j in range(GROUP)
    ]
    for j in range(GROUP):
        pivot = spread_row(columns[j], j)
        inverse = lax.rsqrt(pivot)
        inverse = inverse * (1.5 - 0.5 * pivot * inverse * inverse)
        scale = jnp.where(sub > j, columns[j] * inverse, 0.0)
        for m in range(j + 1, GROUP):
            columns[m] = columns[m] - scale * (spread_row(columns[m], j) * inverse)
        both = jnp.concatenate([inverse, inverse], axis=1)
        scale_both = jnp.concatenate([scale, scale], axis=1)
        scaled = spread_row(rows, j) * both
        rows = jnp.where(sub_wide == j, scaled, rows - scale_both * scaled)
    work_ref[pl.ds(first, GROUP), :] = rows
    later = jnp.where(lanes >= first + GROUP, rows[:, :BLOCK], 0.0)
    work_ref[...] -= exact_dot(later, rows, 0, 0)


def factor_kernel(
    total_rows,
    gram_ref,
    cross_ref,
    factor_ref,
    coupled_ref,
    high_ref,
    low_ref,
    field_ref,
    work_ref,
    inverse_ref,
    weight_ref,
):
    size = gram_ref.shape[0]
    blocks = size // BLOCK
    row_ids = lax.broadcasted_iota(jnp.int32, (BLOCK, BLOCK), 0)
    col_ids = lax.broadcasted_iota(jnp.int32, (BLOCK, BLOCK), 1)
    unit = (row_ids == col_ids).astype(jnp.float32)
    field_ref[:, :size] = gram_ref[...] / total_rows
    field_ref[:, size:] = cross_ref[...] / total_rows
    factor_ref[...] = jnp.zeros_like(factor_ref)
    for b in range(blocks):
        here = slice(b * BLOCK, (b + 1) * BLOCK)
        after = (b + 1) * BLOCK
        work_ref[:, :BLOCK] = field_ref[here, here] + ridge_value * unit
        work_ref[:, BLOCK:] = unit

        def step(group, carry):
            eliminate_group(work_ref, group)
            return carry

        lax.fori_loop(0, BLOCK // GROUP, step, 0)
        factor_ref[here, here] = jnp.where(col_ids >= row_ids, work_ref[:, :BLOCK], 0.0)
        inverse = work_ref[:, BLOCK:]
        inverse_ref[here, :] = inverse
        row_rest = exact_dot(inverse, field_ref[here, after:], 1, 0)
        field_ref[here, after:] = row_rest
        if after < size:
            factor_ref[here, after:] = row_rest[:, : size - after]
            field_ref[after:, after:] -= exact_dot(row_rest[:, : size - after], row_rest, 0, 0)
        coupled_ref[:, here] = row_rest[:, size - after :].T
    for b in range(blocks - 1, -1, -1):
        here = slice(b * BLOCK, (b + 1) * BLOCK)
        after = (b + 1) * BLOCK
        rest = field_ref[here, size:]
        if after < size:
            rest = rest - exact_dot(factor_ref[here, after:], weight_ref[after:, :], 1, 0)
        weight_ref[here, :] = exact_dot(inverse_ref[here, :], rest, 0, 0)
    weights = weight_ref[...]
    high = weights.astype(jnp.bfloat16)
    high_ref[...] = high
    low_ref[...] = (weights - high.astype(jnp.float32)).astype(jnp.bfloat16)


def factor_panel(gram_sum, cross_sum, total_rows):
    size, width = cross_sum.shape
    return pl.pallas_call(
        lambda *refs: factor_kernel(total_rows, *refs),
        out_shape=(
            jax.ShapeDtypeStruct((size, size), jnp.float32),
            jax.ShapeDtypeStruct((width, size), jnp.float32),
            jax.ShapeDtypeStruct((size, width), jnp.bfloat16),
            jax.ShapeDtypeStruct((size, width), jnp.bfloat16),
        ),
        scratch_shapes=[
            pltpu.VMEM((size, size + width), jnp.float32),
            pltpu.VMEM((BLOCK, 2 * BLOCK), jnp.float32),
            pltpu.VMEM((size, BLOCK), jnp.float32),
            pltpu.VMEM((size, width), jnp.float32),
        ],
        compiler_params=pltpu.CompilerParams(vmem_limit_bytes=32 * 1024 * 1024),
        name="factor_panel",
    )(gram_sum, cross_sum)


MESH = pl.DeviceIdType.MESH
VMEM_SPEC = pl.BlockSpec(memory_space=pltpu.VMEM)


def split_axis(count):
    inner = 1
    while 4 * inner * inner <= count:
        inner *= 2
    return count // inner, inner


def here_and_peers(row_count, col_count):
    row, col = lax.axis_index("row"), lax.axis_index("col")
    outer, inner = split_axis(col_count)
    core, lane = row % 2, col % inner
    sibling = row + 1 - 2 * core
    far = [(row, ((col // inner + d) % outer) * inner + lane) for d in range(1, outer)]
    near = [(row, (col // inner) * inner + (lane + e) % inner) for e in range(1, inner)]
    level = [((row + 2 * d) % row_count, col) for d in range(1, row_count // 2)]
    return row, col, core, (sibling, col), far, near, level


def greet(peers):
    barrier = pltpu.get_barrier_semaphore()
    for peer in peers:
        pl.semaphore_signal(barrier, inc=1, device_id=peer, device_id_type=MESH)
    pl.semaphore_wait(barrier, len(peers))


def remote(source, target, send_sem, recv_sem, peer):
    return pltpu.make_async_remote_copy(
        src_ref=source,
        dst_ref=target,
        send_sem=send_sem,
        recv_sem=recv_sem,
        device_id=peer,
        device_id_type=MESH,
    )


def relay(parts, count, place, far_sem, near_sem, side_sem, recv_sem):
    row, col, core, sibling, far, near, _ = place
    started = []

    def send(part, block, sem, peer):
        ref = parts(core, block)[part]
        copy = remote(ref, ref, sem, recv_sem.at[part, core, block], peer)
        copy.start()
        started.append(copy)

    def arrived(part, which, block):
        ref = parts(which, block)[part]
        remote(ref, ref, side_sem.at[part, 0], recv_sem.at[part, which, block], sibling).wait_recv()

    def pass_on(part, block, step):
        for e, peer in enumerate(near):
            send(part, block, near_sem.at[part, step, e], peer)
        send(part, block, side_sem.at[part, step], sibling)

    for part in range(count):
        for d, peer in enumerate(far):
            send(part, col, far_sem.at[part, d], peer)
    for part in range(count):
        pass_on(part, col, 0)
    outer, inner = len(far) + 1, len(near) + 1
    for d in range(1, outer):
        block = far[d - 1][1]
        for part in range(count):
            arrived(part, core, block)
            pass_on(part, block, d)
    home, lane = col // inner, col % inner
    for d in range(outer):
        for e in range(1, inner):
            block = ((home + d) % outer) * inner + (lane + e) % inner
            for part in range(count):
                arrived(part, core, block)
                send(part, block, side_sem.at[part, e * outer + d], sibling)
    for block in range(outer * inner):
        for part in range(count):
            arrived(part, 1 - core, block)
    for copy in started:
        copy.wait_send()


def relay_sems(count, col_count):
    outer, inner = split_axis(col_count)
    return [
        pltpu.SemaphoreType.DMA((count, outer)),
        pltpu.SemaphoreType.DMA((count, outer, inner)),
        pltpu.SemaphoreType.DMA((count, col_count)),
        pltpu.SemaphoreType.DMA((count, 2, col_count)),
    ]


def gather_kernel(
    row_count, col_count, panel_ref, trail_ref, all_ref, own_sem, *sems
):
    place = here_and_peers(row_count, col_count)
    row, col, core, sibling, far, near, _ = place
    panel_width, trail_width = panel_ref.shape[0], trail_ref.shape[0]
    half = panel_ref.shape[1] // 2

    def lanes(which):
        return pl.ds(pl.multiple_of(which * half, half), half)

    def parts(which, block):
        panel_rows = pl.ds(pl.multiple_of(block * panel_width, panel_width), panel_width)
        first = col_count * panel_width + block * trail_width
        trail_rows = pl.ds(pl.multiple_of(first, panel_width), trail_width)
        return [all_ref.at[panel_rows, lanes(which)], all_ref.at[trail_rows, lanes(which)]]

    own = parts(core, col)
    copies = [
        pltpu.make_async_copy(panel_ref.at[:, lanes(core)], own[0], own_sem.at[0]),
        pltpu.make_async_copy(trail_ref.at[:, lanes(core)], own[1], own_sem.at[1]),
    ]
    for copy in copies:
        copy.start()
    greet([sibling, *far, *near])
    for copy in copies:
        copy.wait()
    relay(parts, 2, place, *sems)


def gather_environments(sparse_panel, sparse_trail, row_count, col_count):
    depth = sparse_panel.shape[1]
    width = sparse_panel.shape[0] + sparse_trail.shape[0]
    return pl.pallas_call(
        lambda *refs: gather_kernel(row_count, col_count, *refs),
        out_shape=jax.ShapeDtypeStruct((col_count * width, depth), sparse_panel.dtype),
        in_specs=[VMEM_SPEC] * 2,
        out_specs=VMEM_SPEC,
        scratch_shapes=[pltpu.SemaphoreType.DMA((2,)), *relay_sems(2, col_count)],
        compiler_params=pltpu.CompilerParams(
            collective_id=1, has_side_effects=True, vmem_limit_bytes=32 * 1024 * 1024
        ),
        name="gather_environments",
    )(sparse_panel, sparse_trail)


def exchange_kernel(
    row_count,
    col_count,
    rows_ref,
    panel_ref,
    trail_ref,
    held_ref,
    own_sem,
    row_send,
    row_recv,
    far_send,
    near_send,
    panel_recv,
    trail_send,
    trail_recv,
):
    row, col, core, sibling, far, near, _ = here_and_peers(row_count, col_count)
    panel_total = panel_ref.shape[1]
    trail_width = trail_ref.shape[1]
    slots = rows_ref.shape[0] // row_count
    wide = held_ref.shape[0]
    groups = [(row + d) % row_count for d in range(1, row_count)]
    others = [(col + d) % col_count for d in range(1, col_count)]
    sides = [slice(0, panel_total), slice(panel_total, rows_ref.shape[1])]

    def slot_range(group):
        return pl.ds(pl.multiple_of(group * slots, slots), slots)

    def wide_range(block):
        return pl.ds(pl.multiple_of(block * wide, wide), wide)

    own = pltpu.make_async_copy(
        rows_ref.at[slot_range(row)], held_ref.at[slot_range(row)], own_sem.at[0]
    )
    own.start()
    greet([(group, col) for group in groups] + [(row, other) for other in others])
    started = []

    def send(source, target, send_sem, recv_sem, peer):
        copy = remote(source, target, send_sem, recv_sem, peer)
        copy.start()
        started.append(copy)

    def arrived(target, recv_sem):
        remote(target, target, row_send.at[0, 0], recv_sem, sibling).wait_recv()

    for side, lanes in enumerate(sides):
        for d, group in enumerate(groups):
            send(
                rows_ref.at[slot_range(group), lanes],
                held_ref.at[slot_range(row), lanes],
                row_send.at[side, d],
                row_recv.at[side, row],
                (group, col),
            )
    own.wait()
    for group in groups:
        arrived(held_ref.at[slot_range(group), sides[0]], row_recv.at[0, group])
    mine = held_ref.at[:, sides[0]]
    for d, peer in enumerate(far):
        send(mine, panel_ref.at[wide_range(col)], far_send.at[d], panel_recv.at[col], peer)
    for e, peer in enumerate(near):
        send(mine, panel_ref.at[wide_range(col)], near_send.at[0, e], panel_recv.at[col], peer)
    keep = pltpu.make_async_copy(mine, panel_ref.at[wide_range(col)], own_sem.at[1])
    keep.start()
    for group in groups:
        arrived(held_ref.at[slot_range(group), sides[1]], row_recv.at[1, group])

    def trail_lanes(block):
        first = panel_total + block * trail_width
        return pl.ds(pl.multiple_of(first, trail_width), trail_width)

    for d, other in enumerate(others):
        send(
            held_ref.at[:, trail_lanes(other)],
            trail_ref.at[wide_range(col)],
            trail_send.at[d],
            trail_recv.at[col],
            (row, other),
        )
    keep_trail = pltpu.make_async_copy(
        held_ref.at[:, trail_lanes(col)], trail_ref.at[wide_range(col)], own_sem.at[2]
    )
    keep_trail.start()
    outer, inner = len(far) + 1, len(near) + 1
    for d in range(1, outer):
        block = far[d - 1][1]
        ref = panel_ref.at[wide_range(block)]
        arrived(ref, panel_recv.at[block])
        for e, peer in enumerate(near):
            send(ref, ref, near_send.at[d, e], panel_recv.at[block], peer)
    home, lane = col // inner, col % inner
    for d in range(outer):
        for e in range(1, inner):
            block = ((home + d) % outer) * inner + (lane + e) % inner
            arrived(panel_ref.at[wide_range(block)], panel_recv.at[block])
    for other in others:
        arrived(trail_ref.at[wide_range(other)], trail_recv.at[other])
    keep.wait()
    keep_trail.wait()
    for copy in started:
        copy.wait_send()


def exchange_rows(kernel_rows, panel_total, row_count, col_count):
    total, env_count = kernel_rows.shape
    trail_width = (env_count - panel_total) // col_count
    outer, inner = split_axis(col_count)
    return pl.pallas_call(
        lambda *refs: exchange_kernel(row_count, col_count, *refs),
        out_shape=(
            jax.ShapeDtypeStruct((total * col_count, panel_total), kernel_rows.dtype),
            jax.ShapeDtypeStruct((total * col_count, trail_width), kernel_rows.dtype),
        ),
        in_specs=[VMEM_SPEC],
        out_specs=(VMEM_SPEC, VMEM_SPEC),
        scratch_shapes=[
            pltpu.VMEM((total, env_count), kernel_rows.dtype),
            pltpu.SemaphoreType.DMA((3,)),
            pltpu.SemaphoreType.DMA((2, row_count)),
            pltpu.SemaphoreType.DMA((2, row_count)),
            pltpu.SemaphoreType.DMA((outer,)),
            pltpu.SemaphoreType.DMA((outer, inner)),
            pltpu.SemaphoreType.DMA((col_count,)),
            pltpu.SemaphoreType.DMA((col_count,)),
            pltpu.SemaphoreType.DMA((col_count,)),
        ],
        compiler_params=pltpu.CompilerParams(
            collective_id=3, has_side_effects=True, vmem_limit_bytes=40 * 1024 * 1024
        ),
        name="exchange_rows",
    )(kernel_rows)


def sum_kernel(
    row_count,
    col_count,
    gram_part,
    cross_part,
    gram_ref,
    cross_ref,
    side_ref,
    level_ref,
    side_send,
    side_recv,
    level_send,
    level_recv,
    cross_send,
    cross_recv,
    *sems,
):
    place = here_and_peers(row_count, col_count)
    row, col, core, sibling, far, near, level = place
    gram_half = gram_part.shape[0] // 2
    cross_half = cross_part.shape[0] // 2
    greet([sibling, *far, *near, *level])

    def gram_rows(which):
        return pl.ds(pl.multiple_of(which * gram_half, gram_half), gram_half)

    def cross_rows(which):
        return pl.ds(pl.multiple_of(which * cross_half, cross_half), cross_half)

    to_side = [
        remote(
            gram_part.at[gram_rows(1 - core)],
            side_ref.at[:gram_half],
            side_send.at[0],
            side_recv.at[0],
            sibling,
        ),
        remote(
            cross_part.at[cross_rows(1 - core)],
            side_ref.at[gram_half:],
            side_send.at[1],
            side_recv.at[1],
            sibling,
        ),
    ]
    for copy in to_side:
        copy.start()
    for copy in to_side:
        copy.wait()
    floor = row // 2
    level_ref[floor, :gram_half] = gram_part[gram_rows(core), :] + side_ref[:gram_half]
    level_ref[floor, gram_half:] = cross_part[cross_rows(core), :] + side_ref[gram_half:]
    to_level = []
    for d, peer in enumerate(level):
        mine = level_ref.at[floor]
        copy = remote(mine, mine, level_send.at[d], level_recv.at[floor], peer)
        copy.start()
        to_level.append(copy)
    for d, peer in enumerate(level):
        other = peer[0] // 2
        theirs = level_ref.at[other]
        remote(theirs, theirs, level_send.at[d], level_recv.at[other], peer).wait_recv()
    total = level_ref[0]
    for other in range(1, row_count // 2):
        total = total + level_ref[other]

    def parts(which, block):
        first = block * (2 * gram_half) + which * gram_half
        return [gram_ref.at[pl.ds(pl.multiple_of(first, gram_half), gram_half)]]

    parts(core, col)[0][...] = total[:gram_half]
    cross_ref[cross_rows(core), :] = total[gram_half:]
    mine = cross_ref.at[cross_rows(core)]
    to_cross = remote(mine, mine, cross_send.at[0], cross_recv.at[0], sibling)
    to_cross.start()
    relay(parts, 1, place, *sems)
    to_cross.wait()
    for copy in to_level:
        copy.wait_send()


def sum_products(gram_part, cross_part, row_count, col_count):
    width = gram_part.shape[1]
    half = (gram_part.shape[0] + cross_part.shape[0]) // 2
    levels = row_count // 2
    return pl.pallas_call(
        lambda *refs: sum_kernel(row_count, col_count, *refs),
        out_shape=(
            jax.ShapeDtypeStruct((gram_part.shape[0] * col_count, width), jnp.float32),
            jax.ShapeDtypeStruct(cross_part.shape, jnp.float32),
        ),
        in_specs=[VMEM_SPEC] * 2,
        out_specs=(VMEM_SPEC, VMEM_SPEC),
        scratch_shapes=[
            pltpu.VMEM((half, width), jnp.float32),
            pltpu.VMEM((levels, half, width), jnp.float32),
            pltpu.SemaphoreType.DMA((2,)),
            pltpu.SemaphoreType.DMA((2,)),
            pltpu.SemaphoreType.DMA((levels,)),
            pltpu.SemaphoreType.DMA((levels,)),
            pltpu.SemaphoreType.DMA((1,)),
            pltpu.SemaphoreType.DMA((1,)),
            *relay_sems(1, col_count),
        ],
        compiler_params=pltpu.CompilerParams(
            collective_id=2, has_side_effects=True, vmem_limit_bytes=32 * 1024 * 1024
        ),
        name="sum_products",
    )(gram_part, cross_part)


def contract_rows(left_side, right_side):
    return lax.dot_general(
        left_side, right_side, (((1,), (1,)), ((), ())), preferred_element_type=jnp.float32
    )


def contract_cols(left_side, right_side):
    return lax.dot_general(
        left_side, right_side, (((0,), (0,)), ((), ())), preferred_element_type=jnp.float32
    )


def project(weights, segment):
    return lax.dot_general(
        weights, segment, (((0,), (1,)), ((), ())), preferred_element_type=jnp.float32
    )


def per_device(
    descriptors, gradients, sparse_panel, sparse_trail, atom_counts, owner_rows, neighbor_ids
):
    row_count = lax.axis_size("row")
    col_count = lax.axis_size("col")
    count_here = atom_counts[0]
    owner_here = owner_rows[0]
    slope_here = gradients.reshape(-1, gradients.shape[3])
    panel_width = sparse_panel.shape[0]
    panel_total = panel_width * col_count
    slot_count = 4 * neighbor_ids.shape[1]
    total_rows = row_count * row_count * col_count * slot_count
    environments = gather_environments(sparse_panel, sparse_trail, row_count, col_count)
    kernel_rows = slot_rows(
        environments, descriptors, slope_here, count_here, neighbor_ids, owner_here
    )
    segment, trail_own = exchange_rows(kernel_rows, panel_total, row_count, col_count)
    first = lax.axis_index("col") * panel_width
    panel_own = lax.dynamic_slice_in_dim(segment, first, panel_width, 1)
    gram_sum, cross_sum = sum_products(
        contract_cols(panel_own, segment), contract_cols(trail_own, segment), row_count, col_count
    )
    cross_sum = cross_sum.T
    panel_factor, cross_factor, weight_high, weight_low = factor_panel(
        gram_sum, cross_sum, total_rows
    )
    trail_residual = (
        trail_own.T.astype(jnp.float32)
        - project(weight_high, segment)
        - project(weight_low, segment)
    )
    return (panel_factor, cross_factor, trail_residual)


def solution(mesh):
    return jax.shard_map(
        per_device,
        mesh=mesh,
        in_specs=(
            P(("row", "col"), None),
            P(None, None, ("row", "col"), None),
            P("col", None),
            P("col", None),
            P(("row", "col"), None),
            P(("row", "col"), None),
            P(("row", "col"), None, None),
        ),
        out_specs=(P(), P("col", None), P("col", "row")),
        check_vma=False,
    )
```

```python
import jax
import jax.numpy as jnp
from jax import lax
from jax.experimental import pallas as pl
from jax.experimental.pallas import tpu as pltpu
from jax.sharding import PartitionSpec as P

ridge_value = 0.1


def exact_dot(left_side, right_side, left_dim, right_dim):
    return lax.dot_general(
        left_side,
        right_side,
        (((left_dim,), (right_dim,)), ((), ())),
        preferred_element_type=jnp.float32,
        precision=lax.Precision.HIGHEST,
    )


def slot_rows(environments, desc_here, slope_here, count_here, neighbor_here, owner_here):
    struct_count, atom_slots, neighbor_count = neighbor_here.shape
    env_count = environments.shape[0]
    atoms = struct_count * atom_slots
    correlation = contract_rows(desc_here, environments)
    slope_dots = contract_rows(slope_here, environments)
    slope_dots = slope_dots.reshape(3, neighbor_count, atoms, env_count)
    slot_index = jnp.arange(atom_slots, dtype=jnp.int32)
    live_mask = (slot_index[None, :] < count_here[:, None]).astype(jnp.float32)
    squares = (correlation * correlation).reshape(struct_count, atom_slots, env_count)
    energy = jnp.sum(squares * live_mask[:, :, None], axis=1) / count_here.astype(jnp.float32)[
        :, None
    ]
    partner = neighbor_here % count_here[:, None, None]
    struct_index = jnp.arange(struct_count, dtype=jnp.int32)
    flat_index = struct_index[:, None, None] * atom_slots + partner
    flat_index = jnp.transpose(flat_index.reshape(atoms, neighbor_count))
    atom_index = jnp.arange(atoms, dtype=jnp.int32)
    chooser = jnp.where(
        flat_index[:, :, None] == atom_index, -2.0 * live_mask.reshape(1, atoms, 1), 0.0
    )
    picked = exact_dot(chooser.reshape(neighbor_count * atoms, atoms), correlation, 1, 0)
    picked = picked.reshape(1, neighbor_count, atoms, env_count)
    forces = jnp.sum(picked * slope_dots, axis=1).reshape(3 * atoms, env_count)
    values = jnp.concatenate(
        [energy.astype(jnp.bfloat16), forces.astype(jnp.bfloat16)], axis=0
    )
    chosen = (owner_here[None, :] == struct_index[:, None]).astype(jnp.int32)
    owner_order = jnp.sum(struct_index[None, :] * chosen, axis=1)[:, None]
    slot = jnp.arange(4 * atom_slots, dtype=jnp.int32)[None, :]
    atom, axis = (slot - 1) // 3, (slot - 1) % 3
    source = struct_count + axis * atoms + owner_order * atom_slots + atom
    source = jnp.where(slot <= 3 * atom_slots, source, -1)
    source = jnp.where(slot == 0, owner_order, source).reshape(-1)
    value_index = jnp.arange(values.shape[0], dtype=jnp.int32)
    placing = (source[:, None] == value_index[None, :]).astype(jnp.bfloat16)
    return lax.dot_general(
        placing, values, (((1,), (0,)), ((), ())), preferred_element_type=jnp.float32
    ).astype(jnp.bfloat16)


GROUP = 8
BLOCK = 128


def spread_row(values, row):
    return jnp.broadcast_to(values[row : row + 1, :], values.shape)


def eliminate_group(work_ref, group):
    first = pl.multiple_of(group * GROUP, GROUP)
    rows = work_ref[pl.ds(first, GROUP), :]
    diag = rows[:, :BLOCK]
    lanes = lax.broadcasted_iota(jnp.int32, (GROUP, BLOCK), 1)
    sub = lax.broadcasted_iota(jnp.int32, (GROUP, BLOCK), 0)
    sub_wide = lax.broadcasted_iota(jnp.int32, (GROUP, 2 * BLOCK), 0)
    columns = [
        jnp.broadcast_to(
            jnp.sum(jnp.where(lanes == first + j, diag, 0.0), axis=1, keepdims=True),
            (GROUP, BLOCK),
        )
        for j in range(GROUP)
    ]
    for j in range(GROUP):
        pivot = spread_row(columns[j], j)
        inverse = lax.rsqrt(pivot)
        inverse = inverse * (1.5 - 0.5 * pivot * inverse * inverse)
        scale = jnp.where(sub > j, columns[j] * inverse, 0.0)
        for m in range(j + 1, GROUP):
            columns[m] = columns[m] - scale * (spread_row(columns[m], j) * inverse)
        both = jnp.concatenate([inverse, inverse], axis=1)
        scale_both = jnp.concatenate([scale, scale], axis=1)
        scaled = spread_row(rows, j) * both
        rows = jnp.where(sub_wide == j, scaled, rows - scale_both * scaled)
    work_ref[pl.ds(first, GROUP), :] = rows
    later = jnp.where(lanes >= first + GROUP, rows[:, :BLOCK], 0.0)
    work_ref[...] -= exact_dot(later, rows, 0, 0)


def factor_kernel(
    total_rows,
    gram_ref,
    cross_ref,
    factor_ref,
    coupled_ref,
    high_ref,
    low_ref,
    field_ref,
    work_ref,
    inverse_ref,
    weight_ref,
):
    size = gram_ref.shape[0]
    blocks = size // BLOCK
    row_ids = lax.broadcasted_iota(jnp.int32, (BLOCK, BLOCK), 0)
    col_ids = lax.broadcasted_iota(jnp.int32, (BLOCK, BLOCK), 1)
    unit = (row_ids == col_ids).astype(jnp.float32)
    field_ref[:, :size] = gram_ref[...] / total_rows
    field_ref[:, size:] = cross_ref[...] / total_rows
    factor_ref[...] = jnp.zeros_like(factor_ref)
    for b in range(blocks):
        here = slice(b * BLOCK, (b + 1) * BLOCK)
        after = (b + 1) * BLOCK
        work_ref[:, :BLOCK] = field_ref[here, here] + ridge_value * unit
        work_ref[:, BLOCK:] = unit

        def step(group, carry):
            eliminate_group(work_ref, group)
            return carry

        lax.fori_loop(0, BLOCK // GROUP, step, 0)
        factor_ref[here, here] = jnp.where(col_ids >= row_ids, work_ref[:, :BLOCK], 0.0)
        inverse = work_ref[:, BLOCK:]
        inverse_ref[here, :] = inverse
        row_rest = exact_dot(inverse, field_ref[here, after:], 1, 0)
        field_ref[here, after:] = row_rest
        if after < size:
            factor_ref[here, after:] = row_rest[:, : size - after]
            field_ref[after:, after:] -= exact_dot(row_rest[:, : size - after], row_rest, 0, 0)
        coupled_ref[:, here] = row_rest[:, size - after :].T
    for b in range(blocks - 1, -1, -1):
        here = slice(b * BLOCK, (b + 1) * BLOCK)
        after = (b + 1) * BLOCK
        rest = field_ref[here, size:]
        if after < size:
            rest = rest - exact_dot(factor_ref[here, after:], weight_ref[after:, :], 1, 0)
        weight_ref[here, :] = exact_dot(inverse_ref[here, :], rest, 0, 0)
    weights = weight_ref[...]
    high = weights.astype(jnp.bfloat16)
    high_ref[...] = high
    low_ref[...] = (weights - high.astype(jnp.float32)).astype(jnp.bfloat16)


def factor_panel(gram_sum, cross_sum, total_rows):
    size, width = cross_sum.shape
    return pl.pallas_call(
        lambda *refs: factor_kernel(total_rows, *refs),
        out_shape=(
            jax.ShapeDtypeStruct((size, size), jnp.float32),
            jax.ShapeDtypeStruct((width, size), jnp.float32),
            jax.ShapeDtypeStruct((size, width), jnp.bfloat16),
            jax.ShapeDtypeStruct((size, width), jnp.bfloat16),
        ),
        scratch_shapes=[
            pltpu.VMEM((size, size + width), jnp.float32),
            pltpu.VMEM((BLOCK, 2 * BLOCK), jnp.float32),
            pltpu.VMEM((size, BLOCK), jnp.float32),
            pltpu.VMEM((size, width), jnp.float32),
        ],
        compiler_params=pltpu.CompilerParams(vmem_limit_bytes=32 * 1024 * 1024),
        name="factor_panel",
    )(gram_sum, cross_sum)


MESH = pl.DeviceIdType.MESH
VMEM_SPEC = pl.BlockSpec(memory_space=pltpu.VMEM)


def split_axis(count):
    inner = 1
    while 4 * inner * inner <= count:
        inner *= 2
    return count // inner, inner


def here_and_peers(row_count, col_count):
    row, col = lax.axis_index("row"), lax.axis_index("col")
    outer, inner = split_axis(col_count)
    core, lane = row % 2, col % inner
    sibling = row + 1 - 2 * core
    far = [(row, ((col // inner + d) % outer) * inner + lane) for d in range(1, outer)]
    near = [(row, (col // inner) * inner + (lane + e) % inner) for e in range(1, inner)]
    level = [((row + 2 * d) % row_count, col) for d in range(1, row_count // 2)]
    return row, col, core, (sibling, col), far, near, level


def greet(peers):
    barrier = pltpu.get_barrier_semaphore()
    for peer in peers:
        pl.semaphore_signal(barrier, inc=1, device_id=peer, device_id_type=MESH)
    pl.semaphore_wait(barrier, len(peers))


def remote(source, target, send_sem, recv_sem, peer):
    return pltpu.make_async_remote_copy(
        src_ref=source,
        dst_ref=target,
        send_sem=send_sem,
        recv_sem=recv_sem,
        device_id=peer,
        device_id_type=MESH,
    )


def relay(parts, count, place, far_sem, near_sem, side_sem, recv_sem, pair=True, between=None):
    row, col, core, sibling, far, near, _ = place
    outer, inner = len(far) + 1, len(near) + 1
    home, lane = col // inner, col % inner
    started = []

    def send(part, block, sem, peer, valid=None):
        def build():
            ref = parts(core, block)[part]
            return remote(ref, ref, sem, recv_sem.at[part, core, block], peer)

        started.append((build, valid))
        if valid is None:
            build().start()
        else:
            pl.when(valid)(lambda: build().start())

    def arrived(part, which, block, valid=None):
        def wait():
            ref = parts(which, block)[part]
            sem = recv_sem.at[part, which, block]
            remote(ref, ref, side_sem.at[part, 0], sem, sibling).wait_recv()

        if valid is None:
            wait()
        else:
            pl.when(valid)(wait)

    def both(one, other):
        return one if other is None else jnp.logical_and(one, other)

    def onward(part, block, step, sign, valid=None):
        target = home + sign
        reached = jnp.logical_and(target >= 0, target < outer)
        peer = (row, jnp.clip(target, 0, outer - 1) * inner + lane)
        send(part, block, far_sem.at[part, step], peer, both(reached, valid))

    def pass_on(part, block, step, valid=None):
        for e, peer in enumerate(near):
            send(part, block, near_sem.at[part, step, e], peer, valid)
        if pair:
            send(part, block, side_sem.at[part, step], sibling, valid)

    for part in range(count):
        onward(part, col, 0, -1)
        onward(part, col, 1, 1)
        pass_on(part, col, 0)
    if between is not None:
        between()
    for d in range(1, outer):
        for turn, sign in enumerate((-1, 1)):
            source = home + sign * d
            valid = jnp.logical_and(source >= 0, source < outer)
            block = jnp.clip(source, 0, outer - 1) * inner + lane
            for part in range(count):
                arrived(part, core, block, valid)
                onward(part, block, 2 * d + turn, -sign, valid)
                pass_on(part, block, 2 * d + turn, valid)
    for d in range(outer):
        for e in range(1, inner):
            block = ((home + d) % outer) * inner + (lane + e) % inner
            for part in range(count):
                arrived(part, core, block)
                if pair:
                    send(part, block, side_sem.at[part, 2 * outer + e * outer + d], sibling)
    if pair:
        for block in range(outer * inner):
            for part in range(count):
                arrived(part, 1 - core, block)
    for build, valid in started:
        if valid is None:
            build().wait_send()
        else:
            pl.when(valid)(lambda build=build: build().wait_send())


def relay_sems(count, col_count):
    outer, inner = split_axis(col_count)
    return [
        pltpu.SemaphoreType.DMA((count, 2 * outer)),
        pltpu.SemaphoreType.DMA((count, 2 * outer, inner)),
        pltpu.SemaphoreType.DMA((count, 2 * outer + col_count)),
        pltpu.SemaphoreType.DMA((count, 2, col_count)),
    ]


def gather_kernel(
    row_count, col_count, panel_ref, trail_ref, all_ref, own_sem, *sems
):
    place = here_and_peers(row_count, col_count)
    row, col, core, sibling, far, near, _ = place
    panel_width, trail_width = panel_ref.shape[0], trail_ref.shape[0]
    half = panel_ref.shape[1] // 2

    def lanes(which):
        return pl.ds(pl.multiple_of(which * half, half), half)

    def parts(which, block):
        panel_rows = pl.ds(pl.multiple_of(block * panel_width, panel_width), panel_width)
        first = col_count * panel_width + block * trail_width
        trail_rows = pl.ds(pl.multiple_of(first, panel_width), trail_width)
        return [all_ref.at[panel_rows, lanes(which)], all_ref.at[trail_rows, lanes(which)]]

    own = parts(core, col)
    copies = [
        pltpu.make_async_copy(panel_ref.at[:, lanes(core)], own[0], own_sem.at[0]),
        pltpu.make_async_copy(trail_ref.at[:, lanes(core)], own[1], own_sem.at[1]),
    ]
    for copy in copies:
        copy.start()
    greet([sibling, *far, *near])
    for copy in copies:
        copy.wait()
    relay(parts, 2, place, *sems)


def gather_environments(sparse_panel, sparse_trail, row_count, col_count):
    depth = sparse_panel.shape[1]
    width = sparse_panel.shape[0] + sparse_trail.shape[0]
    return pl.pallas_call(
        lambda *refs: gather_kernel(row_count, col_count, *refs),
        out_shape=jax.ShapeDtypeStruct((col_count * width, depth), sparse_panel.dtype),
        in_specs=[VMEM_SPEC] * 2,
        out_specs=VMEM_SPEC,
        scratch_shapes=[pltpu.SemaphoreType.DMA((2,)), *relay_sems(2, col_count)],
        compiler_params=pltpu.CompilerParams(
            collective_id=1, has_side_effects=True, vmem_limit_bytes=32 * 1024 * 1024
        ),
        name="gather_environments",
    )(sparse_panel, sparse_trail)


def exchange_kernel(
    row_count,
    col_count,
    rows_ref,
    panel_ref,
    trail_ref,
    held_ref,
    own_sem,
    row_send,
    row_recv,
    trail_send,
    trail_recv,
    *sems,
):
    place = here_and_peers(row_count, col_count)
    row, col, core, sibling, far, near, _ = place
    panel_total = panel_ref.shape[1]
    trail_width = trail_ref.shape[1]
    slots = rows_ref.shape[0] // row_count
    wide = held_ref.shape[0]
    groups = [(row + d) % row_count for d in range(1, row_count)]
    others = [(col + d) % col_count for d in range(1, col_count)]
    sides = [slice(0, panel_total), slice(panel_total, rows_ref.shape[1])]

    def slot_range(group):
        return pl.ds(pl.multiple_of(group * slots, slots), slots)

    def wide_range(block):
        return pl.ds(pl.multiple_of(block * wide, wide), wide)

    own = pltpu.make_async_copy(
        rows_ref.at[slot_range(row)], held_ref.at[slot_range(row)], own_sem.at[0]
    )
    own.start()
    greet([(group, col) for group in groups] + [(row, other) for other in others])
    started = []

    def send(source, target, send_sem, recv_sem, peer):
        copy = remote(source, target, send_sem, recv_sem, peer)
        copy.start()
        started.append(copy)

    def arrived(target, recv_sem):
        remote(target, target, row_send.at[0, 0], recv_sem, sibling).wait_recv()

    for side, lanes in enumerate(sides):
        for d, group in enumerate(groups):
            send(
                rows_ref.at[slot_range(group), lanes],
                held_ref.at[slot_range(row), lanes],
                row_send.at[side, d],
                row_recv.at[side, row],
                (group, col),
            )
    own.wait()
    for group in groups:
        arrived(held_ref.at[slot_range(group), sides[0]], row_recv.at[0, group])
    mine = held_ref.at[:, sides[0]]
    keep = pltpu.make_async_copy(mine, panel_ref.at[wide_range(col)], own_sem.at[1])
    keep.start()
    keep.wait()

    def trail_lanes(block):
        first = panel_total + block * trail_width
        return pl.ds(pl.multiple_of(first, trail_width), trail_width)

    keep_trail = pltpu.make_async_copy(
        held_ref.at[:, trail_lanes(col)], trail_ref.at[wide_range(col)], own_sem.at[2]
    )

    def send_trail():
        for group in groups:
            arrived(held_ref.at[slot_range(group), sides[1]], row_recv.at[1, group])
        for d, other in enumerate(others):
            send(
                held_ref.at[:, trail_lanes(other)],
                trail_ref.at[wide_range(col)],
                trail_send.at[d],
                trail_recv.at[col],
                (row, other),
            )
        keep_trail.start()

    def parts(which, block):
        return [panel_ref.at[wide_range(block)]]

    relay(parts, 1, place, *sems, pair=False, between=send_trail)
    for other in others:
        arrived(trail_ref.at[wide_range(other)], trail_recv.at[other])
    keep_trail.wait()
    for copy in started:
        copy.wait_send()


def exchange_rows(kernel_rows, panel_total, row_count, col_count):
    total, env_count = kernel_rows.shape
    trail_width = (env_count - panel_total) // col_count
    return pl.pallas_call(
        lambda *refs: exchange_kernel(row_count, col_count, *refs),
        out_shape=(
            jax.ShapeDtypeStruct((total * col_count, panel_total), kernel_rows.dtype),
            jax.ShapeDtypeStruct((total * col_count, trail_width), kernel_rows.dtype),
        ),
        in_specs=[VMEM_SPEC],
        out_specs=(VMEM_SPEC, VMEM_SPEC),
        scratch_shapes=[
            pltpu.VMEM((total, env_count), kernel_rows.dtype),
            pltpu.SemaphoreType.DMA((3,)),
            pltpu.SemaphoreType.DMA((2, row_count)),
            pltpu.SemaphoreType.DMA((2, row_count)),
            pltpu.SemaphoreType.DMA((col_count,)),
            pltpu.SemaphoreType.DMA((col_count,)),
            *relay_sems(1, col_count),
        ],
        compiler_params=pltpu.CompilerParams(
            collective_id=3, has_side_effects=True, vmem_limit_bytes=40 * 1024 * 1024
        ),
        name="exchange_rows",
    )(kernel_rows)


def sum_kernel(
    row_count,
    col_count,
    gram_part,
    cross_part,
    gram_ref,
    cross_ref,
    side_ref,
    level_ref,
    side_send,
    side_recv,
    level_send,
    level_recv,
    cross_send,
    cross_recv,
    *sems,
):
    place = here_and_peers(row_count, col_count)
    row, col, core, sibling, far, near, level = place
    gram_half = gram_part.shape[0] // 2
    cross_half = cross_part.shape[0] // 2
    greet([sibling, *far, *near, *level])

    def gram_rows(which):
        return pl.ds(pl.multiple_of(which * gram_half, gram_half), gram_half)

    def cross_rows(which):
        return pl.ds(pl.multiple_of(which * cross_half, cross_half), cross_half)

    to_side = [
        remote(
            gram_part.at[gram_rows(1 - core)],
            side_ref.at[:gram_half],
            side_send.at[0],
            side_recv.at[0],
            sibling,
        ),
        remote(
            cross_part.at[cross_rows(1 - core)],
            side_ref.at[gram_half:],
            side_send.at[1],
            side_recv.at[1],
            sibling,
        ),
    ]
    for copy in to_side:
        copy.start()
    for copy in to_side:
        copy.wait()
    floor = row // 2
    level_ref[floor, :gram_half] = gram_part[gram_rows(core), :] + side_ref[:gram_half]
    level_ref[floor, gram_half:] = cross_part[cross_rows(core), :] + side_ref[gram_half:]
    to_level = []
    for d, peer in enumerate(level):
        mine = level_ref.at[floor]
        copy = remote(mine, mine, level_send.at[d], level_recv.at[floor], peer)
        copy.start()
        to_level.append(copy)
    for d, peer in enumerate(level):
        other = peer[0] // 2
        theirs = level_ref.at[other]
        remote(theirs, theirs, level_send.at[d], level_recv.at[other], peer).wait_recv()
    total = level_ref[0]
    for other in range(1, row_count // 2):
        total = total + level_ref[other]

    def parts(which, block):
        first = block * (2 * gram_half) + which * gram_half
        return [gram_ref.at[pl.ds(pl.multiple_of(first, gram_half), gram_half)]]

    parts(core, col)[0][...] = total[:gram_half]
    cross_ref[cross_rows(core), :] = total[gram_half:]
    mine = cross_ref.at[cross_rows(core)]
    to_cross = remote(mine, mine, cross_send.at[0], cross_recv.at[0], sibling)
    to_cross.start()
    relay(parts, 1, place, *sems)
    to_cross.wait()
    for copy in to_level:
        copy.wait_send()


def sum_products(gram_part, cross_part, row_count, col_count):
    width = gram_part.shape[1]
    half = (gram_part.shape[0] + cross_part.shape[0]) // 2
    levels = row_count // 2
    return pl.pallas_call(
        lambda *refs: sum_kernel(row_count, col_count, *refs),
        out_shape=(
            jax.ShapeDtypeStruct((gram_part.shape[0] * col_count, width), jnp.float32),
            jax.ShapeDtypeStruct(cross_part.shape, jnp.float32),
        ),
        in_specs=[VMEM_SPEC] * 2,
        out_specs=(VMEM_SPEC, VMEM_SPEC),
        scratch_shapes=[
            pltpu.VMEM((half, width), jnp.float32),
            pltpu.VMEM((levels, half, width), jnp.float32),
            pltpu.SemaphoreType.DMA((2,)),
            pltpu.SemaphoreType.DMA((2,)),
            pltpu.SemaphoreType.DMA((levels,)),
            pltpu.SemaphoreType.DMA((levels,)),
            pltpu.SemaphoreType.DMA((1,)),
            pltpu.SemaphoreType.DMA((1,)),
            *relay_sems(1, col_count),
        ],
        compiler_params=pltpu.CompilerParams(
            collective_id=2, has_side_effects=True, vmem_limit_bytes=32 * 1024 * 1024
        ),
        name="sum_products",
    )(gram_part, cross_part)


def contract_rows(left_side, right_side):
    return lax.dot_general(
        left_side, right_side, (((1,), (1,)), ((), ())), preferred_element_type=jnp.float32
    )


def contract_cols(left_side, right_side):
    return lax.dot_general(
        left_side, right_side, (((0,), (0,)), ((), ())), preferred_element_type=jnp.float32
    )


def project(weights, segment):
    return lax.dot_general(
        weights, segment, (((0,), (1,)), ((), ())), preferred_element_type=jnp.float32
    )


def per_device(
    descriptors, gradients, sparse_panel, sparse_trail, atom_counts, owner_rows, neighbor_ids
):
    row_count = lax.axis_size("row")
    col_count = lax.axis_size("col")
    count_here = atom_counts[0]
    owner_here = owner_rows[0]
    slope_here = gradients.reshape(-1, gradients.shape[3])
    panel_width = sparse_panel.shape[0]
    panel_total = panel_width * col_count
    slot_count = 4 * neighbor_ids.shape[1]
    total_rows = row_count * row_count * col_count * slot_count
    environments = gather_environments(sparse_panel, sparse_trail, row_count, col_count)
    kernel_rows = slot_rows(
        environments, descriptors, slope_here, count_here, neighbor_ids, owner_here
    )
    segment, trail_own = exchange_rows(kernel_rows, panel_total, row_count, col_count)
    first = lax.axis_index("col") * panel_width
    panel_own = lax.dynamic_slice_in_dim(segment, first, panel_width, 1)
    gram_sum, cross_sum = sum_products(
        contract_cols(panel_own, segment), contract_cols(trail_own, segment), row_count, col_count
    )
    cross_sum = cross_sum.T
    panel_factor, cross_factor, weight_high, weight_low = factor_panel(
        gram_sum, cross_sum, total_rows
    )
    trail_residual = (
        trail_own.T.astype(jnp.float32)
        - project(weight_high, segment)
        - project(weight_low, segment)
    )
    return (panel_factor, cross_factor, trail_residual)


def solution(mesh):
    return jax.shard_map(
        per_device,
        mesh=mesh,
        in_specs=(
            P(("row", "col"), None),
            P(None, None, ("row", "col"), None),
            P("col", None),
            P("col", None),
            P(("row", "col"), None),
            P(("row", "col"), None),
            P(("row", "col"), None, None),
        ),
        out_specs=(P(), P("col", None), P("col", "row")),
        check_vma=False,
    )
```

```python
import jax
import jax.numpy as jnp
from jax import lax
from jax.experimental import pallas as pl
from jax.experimental.pallas import tpu as pltpu
from jax.sharding import PartitionSpec as P

ridge_value = 0.1


def exact_dot(left_side, right_side, left_dim, right_dim):
    return lax.dot_general(
        left_side,
        right_side,
        (((left_dim,), (right_dim,)), ((), ())),
        preferred_element_type=jnp.float32,
        precision=lax.Precision.HIGHEST,
    )


def slot_rows(environments, desc_here, slope_here, count_here, neighbor_here, owner_here):
    struct_count, atom_slots, neighbor_count = neighbor_here.shape
    env_count = environments.shape[0]
    atoms = struct_count * atom_slots
    correlation = contract_rows(desc_here, environments)
    slope_dots = contract_rows(slope_here, environments)
    slope_dots = slope_dots.reshape(3, neighbor_count, atoms, env_count)
    slot_index = jnp.arange(atom_slots, dtype=jnp.int32)
    live_mask = (slot_index[None, :] < count_here[:, None]).astype(jnp.float32)
    squares = (correlation * correlation).reshape(struct_count, atom_slots, env_count)
    energy = jnp.sum(squares * live_mask[:, :, None], axis=1) / count_here.astype(jnp.float32)[
        :, None
    ]
    partner = neighbor_here % count_here[:, None, None]
    struct_index = jnp.arange(struct_count, dtype=jnp.int32)
    flat_index = struct_index[:, None, None] * atom_slots + partner
    flat_index = jnp.transpose(flat_index.reshape(atoms, neighbor_count))
    atom_index = jnp.arange(atoms, dtype=jnp.int32)
    chooser = jnp.where(
        flat_index[:, :, None] == atom_index, -2.0 * live_mask.reshape(1, atoms, 1), 0.0
    )
    picked = exact_dot(chooser.reshape(neighbor_count * atoms, atoms), correlation, 1, 0)
    picked = picked.reshape(1, neighbor_count, atoms, env_count)
    forces = jnp.sum(picked * slope_dots, axis=1).reshape(3 * atoms, env_count)
    values = jnp.concatenate(
        [energy.astype(jnp.bfloat16), forces.astype(jnp.bfloat16)], axis=0
    )
    chosen = (owner_here[None, :] == struct_index[:, None]).astype(jnp.int32)
    owner_order = jnp.sum(struct_index[None, :] * chosen, axis=1)[:, None]
    slot = jnp.arange(4 * atom_slots, dtype=jnp.int32)[None, :]
    atom, axis = (slot - 1) // 3, (slot - 1) % 3
    source = struct_count + axis * atoms + owner_order * atom_slots + atom
    source = jnp.where(slot <= 3 * atom_slots, source, -1)
    source = jnp.where(slot == 0, owner_order, source).reshape(-1)
    value_index = jnp.arange(values.shape[0], dtype=jnp.int32)
    placing = (source[:, None] == value_index[None, :]).astype(jnp.bfloat16)
    return lax.dot_general(
        placing, values, (((1,), (0,)), ((), ())), preferred_element_type=jnp.float32
    ).astype(jnp.bfloat16)


GROUP = 16
BLOCK = 128


def spread_row(values, row):
    return jnp.broadcast_to(values[row : row + 1, :], values.shape)


def eliminate_group(work_ref, group):
    first = pl.multiple_of(group * GROUP, GROUP)
    rows = work_ref[pl.ds(first, GROUP), :]
    diag = rows[:, :BLOCK]
    lanes = lax.broadcasted_iota(jnp.int32, (GROUP, BLOCK), 1)
    sub = lax.broadcasted_iota(jnp.int32, (GROUP, BLOCK), 0)
    sub_wide = lax.broadcasted_iota(jnp.int32, (GROUP, 2 * BLOCK), 0)
    columns = [
        jnp.broadcast_to(
            jnp.sum(jnp.where(lanes == first + j, diag, 0.0), axis=1, keepdims=True),
            (GROUP, BLOCK),
        )
        for j in range(GROUP)
    ]
    for j in range(GROUP):
        pivot = spread_row(columns[j], j)
        inverse = lax.rsqrt(pivot)
        inverse = inverse * (1.5 - 0.5 * pivot * inverse * inverse)
        scale = jnp.where(sub > j, columns[j] * inverse, 0.0)
        for m in range(j + 1, GROUP):
            columns[m] = columns[m] - scale * (spread_row(columns[m], j) * inverse)
        both = jnp.concatenate([inverse, inverse], axis=1)
        scale_both = jnp.concatenate([scale, scale], axis=1)
        scaled = spread_row(rows, j) * both
        rows = jnp.where(sub_wide == j, scaled, rows - scale_both * scaled)
    work_ref[pl.ds(first, GROUP), :] = rows
    later = jnp.where(lanes >= first + GROUP, rows[:, :BLOCK], 0.0)
    work_ref[...] -= exact_dot(later, rows, 0, 0)


def factor_kernel(
    total_rows,
    gram_ref,
    cross_ref,
    factor_ref,
    coupled_ref,
    high_ref,
    low_ref,
    field_ref,
    work_ref,
    inverse_ref,
    weight_ref,
):
    size = gram_ref.shape[0]
    blocks = size // BLOCK
    row_ids = lax.broadcasted_iota(jnp.int32, (BLOCK, BLOCK), 0)
    col_ids = lax.broadcasted_iota(jnp.int32, (BLOCK, BLOCK), 1)
    unit = (row_ids == col_ids).astype(jnp.float32)
    field_ref[:, :size] = gram_ref[...] / total_rows
    field_ref[:, size:] = cross_ref[...].T / total_rows
    factor_ref[...] = jnp.zeros_like(factor_ref)
    for b in range(blocks):
        here = slice(b * BLOCK, (b + 1) * BLOCK)
        after = (b + 1) * BLOCK
        work_ref[:, :BLOCK] = field_ref[here, here] + ridge_value * unit
        work_ref[:, BLOCK:] = unit

        def step(group, carry):
            eliminate_group(work_ref, group)
            return carry

        lax.fori_loop(0, BLOCK // GROUP, step, 0)
        factor_ref[here, here] = jnp.where(col_ids >= row_ids, work_ref[:, :BLOCK], 0.0)
        inverse = work_ref[:, BLOCK:]
        inverse_ref[here, :] = inverse
        row_rest = exact_dot(inverse, field_ref[here, after:], 1, 0)
        field_ref[here, after:] = row_rest
        if after < size:
            factor_ref[here, after:] = row_rest[:, : size - after]
            field_ref[after:, after:] -= exact_dot(row_rest[:, : size - after], row_rest, 0, 0)
        coupled_ref[:, here] = row_rest[:, size - after :].T
    for b in range(blocks - 1, -1, -1):
        here = slice(b * BLOCK, (b + 1) * BLOCK)
        after = (b + 1) * BLOCK
        rest = field_ref[here, size:]
        if after < size:
            rest = rest - exact_dot(factor_ref[here, after:], weight_ref[after:, :], 1, 0)
        weight_ref[here, :] = exact_dot(inverse_ref[here, :], rest, 0, 0)
    weights = weight_ref[...]
    high = weights.astype(jnp.bfloat16)
    high_ref[...] = high
    low_ref[...] = (weights - high.astype(jnp.float32)).astype(jnp.bfloat16)


def factor_panel(gram_sum, cross_sum, total_rows):
    width, size = cross_sum.shape
    return pl.pallas_call(
        lambda *refs: factor_kernel(total_rows, *refs),
        out_shape=(
            jax.ShapeDtypeStruct((size, size), jnp.float32),
            jax.ShapeDtypeStruct((width, size), jnp.float32),
            jax.ShapeDtypeStruct((size, width), jnp.bfloat16),
            jax.ShapeDtypeStruct((size, width), jnp.bfloat16),
        ),
        scratch_shapes=[
            pltpu.VMEM((size, size + width), jnp.float32),
            pltpu.VMEM((BLOCK, 2 * BLOCK), jnp.float32),
            pltpu.VMEM((size, BLOCK), jnp.float32),
            pltpu.VMEM((size, width), jnp.float32),
        ],
        compiler_params=pltpu.CompilerParams(vmem_limit_bytes=32 * 1024 * 1024),
        name="factor_panel",
    )(gram_sum, cross_sum)


MESH = pl.DeviceIdType.MESH
VMEM_SPEC = pl.BlockSpec(memory_space=pltpu.VMEM)


def split_axis(count):
    inner = 1
    while 4 * inner * inner <= count:
        inner *= 2
    return count // inner, inner


def here_and_peers(row_count, col_count):
    row, col = lax.axis_index("row"), lax.axis_index("col")
    outer, inner = split_axis(col_count)
    core, lane = row % 2, col % inner
    sibling = row + 1 - 2 * core
    far = [(row, ((col // inner + d) % outer) * inner + lane) for d in range(1, outer)]
    near = [(row, (col // inner) * inner + (lane + e) % inner) for e in range(1, inner)]
    level = [((row + 2 * d) % row_count, col) for d in range(1, row_count // 2)]
    return row, col, core, (sibling, col), far, near, level


def greet(peers):
    barrier = pltpu.get_barrier_semaphore()
    for peer in peers:
        pl.semaphore_signal(barrier, inc=1, device_id=peer, device_id_type=MESH)
    pl.semaphore_wait(barrier, len(peers))


def remote(source, target, send_sem, recv_sem, peer):
    return pltpu.make_async_remote_copy(
        src_ref=source,
        dst_ref=target,
        send_sem=send_sem,
        recv_sem=recv_sem,
        device_id=peer,
        device_id_type=MESH,
    )


def relay(parts, count, place, far_sem, near_sem, side_sem, recv_sem, pair=True, between=None):
    row, col, core, sibling, far, near, _ = place
    outer, inner = len(far) + 1, len(near) + 1
    home, lane = col // inner, col % inner
    started = []

    def send(part, block, sem, peer, valid=None):
        def build():
            ref = parts(core, block)[part]
            return remote(ref, ref, sem, recv_sem.at[part, core, block], peer)

        started.append((build, valid))
        if valid is None:
            build().start()
        else:
            pl.when(valid)(lambda: build().start())

    def arrived(part, which, block, valid=None):
        def wait():
            ref = parts(which, block)[part]
            sem = recv_sem.at[part, which, block]
            remote(ref, ref, side_sem.at[part, 0], sem, sibling).wait_recv()

        if valid is None:
            wait()
        else:
            pl.when(valid)(wait)

    def both(one, other):
        return one if other is None else jnp.logical_and(one, other)

    def onward(part, block, step, sign, valid=None):
        target = home + sign
        reached = jnp.logical_and(target >= 0, target < outer)
        peer = (row, jnp.clip(target, 0, outer - 1) * inner + lane)
        send(part, block, far_sem.at[part, step], peer, both(reached, valid))

    def pass_on(part, block, step, valid=None):
        for e, peer in enumerate(near):
            send(part, block, near_sem.at[part, step, e], peer, valid)
        if pair:
            send(part, block, side_sem.at[part, step], sibling, valid)

    for part in range(count):
        onward(part, col, 0, -1)
        onward(part, col, 1, 1)
        pass_on(part, col, 0)
    if between is not None:
        between()
    for d in range(1, outer):
        for turn, sign in enumerate((-1, 1)):
            source = home + sign * d
            valid = jnp.logical_and(source >= 0, source < outer)
            block = jnp.clip(source, 0, outer - 1) * inner + lane
            for part in range(count):
                arrived(part, core, block, valid)
                onward(part, block, 2 * d + turn, -sign, valid)
                pass_on(part, block, 2 * d + turn, valid)
    for d in range(outer):
        for e in range(1, inner):
            block = ((home + d) % outer) * inner + (lane + e) % inner
            for part in range(count):
                arrived(part, core, block)
                if pair:
                    send(part, block, side_sem.at[part, 2 * outer + e * outer + d], sibling)
    if pair:
        for block in range(outer * inner):
            for part in range(count):
                arrived(part, 1 - core, block)
    for build, valid in started:
        if valid is None:
            build().wait_send()
        else:
            pl.when(valid)(lambda build=build: build().wait_send())


def relay_sems(count, col_count):
    outer, inner = split_axis(col_count)
    return [
        pltpu.SemaphoreType.DMA((count, 2 * outer)),
        pltpu.SemaphoreType.DMA((count, 2 * outer, inner)),
        pltpu.SemaphoreType.DMA((count, 2 * outer + col_count)),
        pltpu.SemaphoreType.DMA((count, 2, col_count)),
    ]


def gather_kernel(
    row_count, col_count, panel_ref, trail_ref, all_ref, own_sem, *sems
):
    place = here_and_peers(row_count, col_count)
    row, col, core, sibling, far, near, _ = place
    panel_width, trail_width = panel_ref.shape[0], trail_ref.shape[0]
    half = panel_ref.shape[1] // 2

    def lanes(which):
        return pl.ds(pl.multiple_of(which * half, half), half)

    def parts(which, block):
        panel_rows = pl.ds(pl.multiple_of(block * panel_width, panel_width), panel_width)
        first = col_count * panel_width + block * trail_width
        trail_rows = pl.ds(pl.multiple_of(first, panel_width), trail_width)
        return [all_ref.at[panel_rows, lanes(which)], all_ref.at[trail_rows, lanes(which)]]

    own = parts(core, col)
    copies = [
        pltpu.make_async_copy(panel_ref.at[:, lanes(core)], own[0], own_sem.at[0]),
        pltpu.make_async_copy(trail_ref.at[:, lanes(core)], own[1], own_sem.at[1]),
    ]
    for copy in copies:
        copy.start()
    greet([sibling, *far, *near])
    for copy in copies:
        copy.wait()
    relay(parts, 2, place, *sems)


def gather_environments(sparse_panel, sparse_trail, row_count, col_count):
    depth = sparse_panel.shape[1]
    width = sparse_panel.shape[0] + sparse_trail.shape[0]
    return pl.pallas_call(
        lambda *refs: gather_kernel(row_count, col_count, *refs),
        out_shape=jax.ShapeDtypeStruct((col_count * width, depth), sparse_panel.dtype),
        in_specs=[VMEM_SPEC] * 2,
        out_specs=VMEM_SPEC,
        scratch_shapes=[pltpu.SemaphoreType.DMA((2,)), *relay_sems(2, col_count)],
        compiler_params=pltpu.CompilerParams(
            collective_id=1, has_side_effects=True, vmem_limit_bytes=32 * 1024 * 1024
        ),
        name="gather_environments",
    )(sparse_panel, sparse_trail)


def exchange_kernel(
    row_count,
    col_count,
    rows_ref,
    panel_ref,
    trail_ref,
    held_ref,
    own_sem,
    row_send,
    row_recv,
    trail_send,
    trail_recv,
    *sems,
):
    place = here_and_peers(row_count, col_count)
    row, col, core, sibling, far, near, _ = place
    panel_total = panel_ref.shape[1]
    trail_width = trail_ref.shape[1]
    slots = rows_ref.shape[0] // row_count
    wide = held_ref.shape[0]
    groups = [(row + d) % row_count for d in range(1, row_count)]
    others = [(col + d) % col_count for d in range(1, col_count)]
    sides = [slice(0, panel_total), slice(panel_total, rows_ref.shape[1])]

    def slot_range(group):
        return pl.ds(pl.multiple_of(group * slots, slots), slots)

    def wide_range(block):
        return pl.ds(pl.multiple_of(block * wide, wide), wide)

    own = pltpu.make_async_copy(
        rows_ref.at[slot_range(row)], held_ref.at[slot_range(row)], own_sem.at[0]
    )
    own.start()
    greet([(group, col) for group in groups] + [(row, other) for other in others])
    started = []

    def send(source, target, send_sem, recv_sem, peer):
        copy = remote(source, target, send_sem, recv_sem, peer)
        copy.start()
        started.append(copy)

    def arrived(target, recv_sem):
        remote(target, target, row_send.at[0, 0], recv_sem, sibling).wait_recv()

    for side, lanes in enumerate(sides):
        for d, group in enumerate(groups):
            send(
                rows_ref.at[slot_range(group), lanes],
                held_ref.at[slot_range(row), lanes],
                row_send.at[side, d],
                row_recv.at[side, row],
                (group, col),
            )
    own.wait()
    for group in groups:
        arrived(held_ref.at[slot_range(group), sides[0]], row_recv.at[0, group])
    mine = held_ref.at[:, sides[0]]
    keep = pltpu.make_async_copy(mine, panel_ref.at[wide_range(col)], own_sem.at[1])
    keep.start()
    keep.wait()

    def trail_lanes(block):
        first = panel_total + block * trail_width
        return pl.ds(pl.multiple_of(first, trail_width), trail_width)

    keep_trail = pltpu.make_async_copy(
        held_ref.at[:, trail_lanes(col)], trail_ref.at[wide_range(col)], own_sem.at[2]
    )

    def send_trail():
        for group in groups:
            arrived(held_ref.at[slot_range(group), sides[1]], row_recv.at[1, group])
        for d, other in enumerate(others):
            send(
                held_ref.at[:, trail_lanes(other)],
                trail_ref.at[wide_range(col)],
                trail_send.at[d],
                trail_recv.at[col],
                (row, other),
            )
        keep_trail.start()

    def parts(which, block):
        return [panel_ref.at[wide_range(block)]]

    relay(parts, 1, place, *sems, pair=False, between=send_trail)
    for other in others:
        arrived(trail_ref.at[wide_range(other)], trail_recv.at[other])
    keep_trail.wait()
    for copy in started:
        copy.wait_send()


def exchange_rows(kernel_rows, panel_total, row_count, col_count):
    total, env_count = kernel_rows.shape
    trail_width = (env_count - panel_total) // col_count
    return pl.pallas_call(
        lambda *refs: exchange_kernel(row_count, col_count, *refs),
        out_shape=(
            jax.ShapeDtypeStruct((total * col_count, panel_total), kernel_rows.dtype),
            jax.ShapeDtypeStruct((total * col_count, trail_width), kernel_rows.dtype),
        ),
        in_specs=[VMEM_SPEC],
        out_specs=(VMEM_SPEC, VMEM_SPEC),
        scratch_shapes=[
            pltpu.VMEM((total, env_count), kernel_rows.dtype),
            pltpu.SemaphoreType.DMA((3,)),
            pltpu.SemaphoreType.DMA((2, row_count)),
            pltpu.SemaphoreType.DMA((2, row_count)),
            pltpu.SemaphoreType.DMA((col_count,)),
            pltpu.SemaphoreType.DMA((col_count,)),
            *relay_sems(1, col_count),
        ],
        compiler_params=pltpu.CompilerParams(
            collective_id=3, has_side_effects=True, vmem_limit_bytes=40 * 1024 * 1024
        ),
        name="exchange_rows",
    )(kernel_rows)


def sum_kernel(
    row_count,
    col_count,
    gram_part,
    cross_part,
    gram_ref,
    cross_ref,
    side_ref,
    level_ref,
    side_send,
    side_recv,
    level_send,
    level_recv,
    cross_send,
    cross_recv,
    *sems,
):
    place = here_and_peers(row_count, col_count)
    row, col, core, sibling, far, near, level = place
    gram_half = gram_part.shape[0] // 2
    cross_half = cross_part.shape[0] // 2
    greet([sibling, *far, *near, *level])

    def gram_rows(which):
        return pl.ds(pl.multiple_of(which * gram_half, gram_half), gram_half)

    def cross_rows(which):
        return pl.ds(pl.multiple_of(which * cross_half, cross_half), cross_half)

    to_side = [
        remote(
            gram_part.at[gram_rows(1 - core)],
            side_ref.at[:gram_half],
            side_send.at[0],
            side_recv.at[0],
            sibling,
        ),
        remote(
            cross_part.at[cross_rows(1 - core)],
            side_ref.at[gram_half:],
            side_send.at[1],
            side_recv.at[1],
            sibling,
        ),
    ]
    for copy in to_side:
        copy.start()
    for copy in to_side:
        copy.wait()
    floor = row // 2
    level_ref[floor, :gram_half] = gram_part[gram_rows(core), :] + side_ref[:gram_half]
    level_ref[floor, gram_half:] = cross_part[cross_rows(core), :] + side_ref[gram_half:]
    to_level = []
    for d, peer in enumerate(level):
        mine = level_ref.at[floor]
        copy = remote(mine, mine, level_send.at[d], level_recv.at[floor], peer)
        copy.start()
        to_level.append(copy)
    for d, peer in enumerate(level):
        other = peer[0] // 2
        theirs = level_ref.at[other]
        remote(theirs, theirs, level_send.at[d], level_recv.at[other], peer).wait_recv()
    total = level_ref[0]
    for other in range(1, row_count // 2):
        total = total + level_ref[other]

    def parts(which, block):
        first = block * (2 * gram_half) + which * gram_half
        return [gram_ref.at[pl.ds(pl.multiple_of(first, gram_half), gram_half)]]

    parts(core, col)[0][...] = total[:gram_half]
    cross_ref[cross_rows(core), :] = total[gram_half:]
    mine = cross_ref.at[cross_rows(core)]
    to_cross = remote(mine, mine, cross_send.at[0], cross_recv.at[0], sibling)
    to_cross.start()
    relay(parts, 1, place, *sems)
    to_cross.wait()
    for copy in to_level:
        copy.wait_send()


def sum_products(gram_part, cross_part, row_count, col_count):
    width = gram_part.shape[1]
    half = (gram_part.shape[0] + cross_part.shape[0]) // 2
    levels = row_count // 2
    return pl.pallas_call(
        lambda *refs: sum_kernel(row_count, col_count, *refs),
        out_shape=(
            jax.ShapeDtypeStruct((gram_part.shape[0] * col_count, width), jnp.float32),
            jax.ShapeDtypeStruct(cross_part.shape, jnp.float32),
        ),
        in_specs=[VMEM_SPEC] * 2,
        out_specs=(VMEM_SPEC, VMEM_SPEC),
        scratch_shapes=[
            pltpu.VMEM((half, width), jnp.float32),
            pltpu.VMEM((levels, half, width), jnp.float32),
            pltpu.SemaphoreType.DMA((2,)),
            pltpu.SemaphoreType.DMA((2,)),
            pltpu.SemaphoreType.DMA((levels,)),
            pltpu.SemaphoreType.DMA((levels,)),
            pltpu.SemaphoreType.DMA((1,)),
            pltpu.SemaphoreType.DMA((1,)),
            *relay_sems(1, col_count),
        ],
        compiler_params=pltpu.CompilerParams(
            collective_id=2, has_side_effects=True, vmem_limit_bytes=32 * 1024 * 1024
        ),
        name="sum_products",
    )(gram_part, cross_part)


def contract_rows(left_side, right_side):
    return lax.dot_general(
        left_side, right_side, (((1,), (1,)), ((), ())), preferred_element_type=jnp.float32
    )


def contract_cols(left_side, right_side):
    return lax.dot_general(
        left_side, right_side, (((0,), (0,)), ((), ())), preferred_element_type=jnp.float32
    )


def project(weights, segment):
    return lax.dot_general(
        weights, segment, (((0,), (1,)), ((), ())), preferred_element_type=jnp.float32
    )


def per_device(
    descriptors, gradients, sparse_panel, sparse_trail, atom_counts, owner_rows, neighbor_ids
):
    row_count = lax.axis_size("row")
    col_count = lax.axis_size("col")
    count_here = atom_counts[0]
    owner_here = owner_rows[0]
    slope_here = gradients.reshape(-1, gradients.shape[3])
    panel_width = sparse_panel.shape[0]
    panel_total = panel_width * col_count
    slot_count = 4 * neighbor_ids.shape[1]
    total_rows = row_count * row_count * col_count * slot_count
    environments = gather_environments(sparse_panel, sparse_trail, row_count, col_count)
    kernel_rows = slot_rows(
        environments, descriptors, slope_here, count_here, neighbor_ids, owner_here
    )
    segment, trail_own = exchange_rows(kernel_rows, panel_total, row_count, col_count)
    first = lax.axis_index("col") * panel_width
    panel_own = lax.dynamic_slice_in_dim(segment, first, panel_width, 1)
    gram_sum, cross_sum = sum_products(
        contract_cols(panel_own, segment), contract_cols(trail_own, segment), row_count, col_count
    )
    panel_factor, cross_factor, weight_high, weight_low = factor_panel(
        gram_sum, cross_sum, total_rows
    )
    trail_residual = (
        trail_own.T.astype(jnp.float32)
        - project(weight_high, segment)
        - project(weight_low, segment)
    )
    return (panel_factor, cross_factor, trail_residual)


def solution(mesh):
    return jax.shard_map(
        per_device,
        mesh=mesh,
        in_specs=(
            P(("row", "col"), None),
            P(None, None, ("row", "col"), None),
            P("col", None),
            P("col", None),
            P(("row", "col"), None),
            P(("row", "col"), None),
            P(("row", "col"), None, None),
        ),
        out_specs=(P(), P("col", None), P("col", "row")),
        check_vma=False,
    )
```

```python
import jax
import jax.numpy as jnp
from jax import lax
from jax.experimental import pallas as pl
from jax.experimental.pallas import tpu as pltpu
from jax.sharding import PartitionSpec as P

ridge_value = 0.1


def exact_dot(left_side, right_side, left_dim, right_dim):
    return lax.dot_general(
        left_side,
        right_side,
        (((left_dim,), (right_dim,)), ((), ())),
        preferred_element_type=jnp.float32,
        precision=lax.Precision.HIGHEST,
    )


def slot_rows(environments, desc_here, slope_here, count_here, neighbor_here, owner_here):
    struct_count, atom_slots, neighbor_count = neighbor_here.shape
    env_count = environments.shape[0]
    atoms = struct_count * atom_slots
    correlation = contract_rows(desc_here, environments)
    slope_dots = contract_rows(slope_here, environments)
    slope_dots = slope_dots.reshape(3, neighbor_count, atoms, env_count)
    slot_index = jnp.arange(atom_slots, dtype=jnp.int32)
    live_mask = (slot_index[None, :] < count_here[:, None]).astype(jnp.float32)
    squares = (correlation * correlation).reshape(struct_count, atom_slots, env_count)
    energy = jnp.sum(squares * live_mask[:, :, None], axis=1) / count_here.astype(jnp.float32)[
        :, None
    ]
    partner = neighbor_here % count_here[:, None, None]
    struct_index = jnp.arange(struct_count, dtype=jnp.int32)
    flat_index = struct_index[:, None, None] * atom_slots + partner
    flat_index = jnp.transpose(flat_index.reshape(atoms, neighbor_count))
    atom_index = jnp.arange(atoms, dtype=jnp.int32)
    chooser = jnp.where(
        flat_index[:, :, None] == atom_index, -2.0 * live_mask.reshape(1, atoms, 1), 0.0
    )
    picked = exact_dot(chooser.reshape(neighbor_count * atoms, atoms), correlation, 1, 0)
    picked = picked.reshape(1, neighbor_count, atoms, env_count)
    forces = jnp.sum(picked * slope_dots, axis=1).reshape(3 * atoms, env_count)
    values = jnp.concatenate(
        [energy.astype(jnp.bfloat16), forces.astype(jnp.bfloat16)], axis=0
    )
    chosen = (owner_here[None, :] == struct_index[:, None]).astype(jnp.int32)
    owner_order = jnp.sum(struct_index[None, :] * chosen, axis=1)[:, None]
    slot = jnp.arange(4 * atom_slots, dtype=jnp.int32)[None, :]
    atom, axis = (slot - 1) // 3, (slot - 1) % 3
    source = struct_count + axis * atoms + owner_order * atom_slots + atom
    source = jnp.where(slot <= 3 * atom_slots, source, -1)
    source = jnp.where(slot == 0, owner_order, source).reshape(-1)
    value_index = jnp.arange(values.shape[0], dtype=jnp.int32)
    placing = (source[:, None] == value_index[None, :]).astype(jnp.bfloat16)
    return lax.dot_general(
        placing, values, (((1,), (0,)), ((), ())), preferred_element_type=jnp.float32
    ).astype(jnp.bfloat16)


GROUP = 32
BLOCK = 128


def spread_row(values, row):
    return jnp.broadcast_to(values[row : row + 1, :], values.shape)


def eliminate_group(work_ref, group):
    first = pl.multiple_of(group * GROUP, GROUP)
    rows = work_ref[pl.ds(first, GROUP), :]
    diag = rows[:, :BLOCK]
    lanes = lax.broadcasted_iota(jnp.int32, (GROUP, BLOCK), 1)
    sub = lax.broadcasted_iota(jnp.int32, (GROUP, BLOCK), 0)
    sub_wide = lax.broadcasted_iota(jnp.int32, (GROUP, 2 * BLOCK), 0)
    columns = [
        jnp.broadcast_to(
            jnp.sum(jnp.where(lanes == first + j, diag, 0.0), axis=1, keepdims=True),
            (GROUP, BLOCK),
        )
        for j in range(GROUP)
    ]
    for j in range(GROUP):
        pivot = spread_row(columns[j], j)
        inverse = lax.rsqrt(pivot)
        inverse = inverse * (1.5 - 0.5 * pivot * inverse * inverse)
        scale = jnp.where(sub > j, columns[j] * inverse, 0.0)
        for m in range(j + 1, GROUP):
            columns[m] = columns[m] - scale * (spread_row(columns[m], j) * inverse)
        both = jnp.concatenate([inverse, inverse], axis=1)
        scale_both = jnp.concatenate([scale, scale], axis=1)
        scaled = spread_row(rows, j) * both
        rows = jnp.where(sub_wide == j, scaled, rows - scale_both * scaled)
    work_ref[pl.ds(first, GROUP), :] = rows
    later = jnp.where(lanes >= first + GROUP, rows[:, :BLOCK], 0.0)
    work_ref[...] -= exact_dot(later, rows, 0, 0)


def factor_kernel(
    total_rows,
    gram_ref,
    cross_ref,
    factor_ref,
    coupled_ref,
    high_ref,
    low_ref,
    field_ref,
    work_ref,
    inverse_ref,
    weight_ref,
):
    size = gram_ref.shape[0]
    blocks = size // BLOCK
    row_ids = lax.broadcasted_iota(jnp.int32, (BLOCK, BLOCK), 0)
    col_ids = lax.broadcasted_iota(jnp.int32, (BLOCK, BLOCK), 1)
    unit = (row_ids == col_ids).astype(jnp.float32)
    field_ref[:, :size] = gram_ref[...] / total_rows
    field_ref[:, size:] = cross_ref[...].T / total_rows
    factor_ref[...] = jnp.zeros_like(factor_ref)
    for b in range(blocks):
        here = slice(b * BLOCK, (b + 1) * BLOCK)
        after = (b + 1) * BLOCK
        work_ref[:, :BLOCK] = field_ref[here, here] + ridge_value * unit
        work_ref[:, BLOCK:] = unit

        def step(group, carry):
            eliminate_group(work_ref, group)
            return carry

        lax.fori_loop(0, BLOCK // GROUP, step, 0)
        factor_ref[here, here] = jnp.where(col_ids >= row_ids, work_ref[:, :BLOCK], 0.0)
        inverse = work_ref[:, BLOCK:]
        inverse_ref[here, :] = inverse
        row_rest = exact_dot(inverse, field_ref[here, after:], 1, 0)
        field_ref[here, after:] = row_rest
        if after < size:
            factor_ref[here, after:] = row_rest[:, : size - after]
            field_ref[after:, after:] -= exact_dot(row_rest[:, : size - after], row_rest, 0, 0)
        coupled_ref[:, here] = row_rest[:, size - after :].T
    for b in range(blocks - 1, -1, -1):
        here = slice(b * BLOCK, (b + 1) * BLOCK)
        after = (b + 1) * BLOCK
        rest = field_ref[here, size:]
        if after < size:
            rest = rest - exact_dot(factor_ref[here, after:], weight_ref[after:, :], 1, 0)
        weight_ref[here, :] = exact_dot(inverse_ref[here, :], rest, 0, 0)
    weights = weight_ref[...]
    high = weights.astype(jnp.bfloat16)
    high_ref[...] = high
    low_ref[...] = (weights - high.astype(jnp.float32)).astype(jnp.bfloat16)


def factor_panel(gram_sum, cross_sum, total_rows):
    width, size = cross_sum.shape
    return pl.pallas_call(
        lambda *refs: factor_kernel(total_rows, *refs),
        out_shape=(
            jax.ShapeDtypeStruct((size, size), jnp.float32),
            jax.ShapeDtypeStruct((width, size), jnp.float32),
            jax.ShapeDtypeStruct((size, width), jnp.bfloat16),
            jax.ShapeDtypeStruct((size, width), jnp.bfloat16),
        ),
        scratch_shapes=[
            pltpu.VMEM((size, size + width), jnp.float32),
            pltpu.VMEM((BLOCK, 2 * BLOCK), jnp.float32),
            pltpu.VMEM((size, BLOCK), jnp.float32),
            pltpu.VMEM((size, width), jnp.float32),
        ],
        compiler_params=pltpu.CompilerParams(vmem_limit_bytes=32 * 1024 * 1024),
        name="factor_panel",
    )(gram_sum, cross_sum)


MESH = pl.DeviceIdType.MESH
VMEM_SPEC = pl.BlockSpec(memory_space=pltpu.VMEM)


def split_axis(count):
    inner = 1
    while 4 * inner * inner <= count:
        inner *= 2
    return count // inner, inner


def here_and_peers(row_count, col_count):
    row, col = lax.axis_index("row"), lax.axis_index("col")
    outer, inner = split_axis(col_count)
    core, lane = row % 2, col % inner
    sibling = row + 1 - 2 * core
    far = [(row, ((col // inner + d) % outer) * inner + lane) for d in range(1, outer)]
    near = [(row, (col // inner) * inner + (lane + e) % inner) for e in range(1, inner)]
    level = [((row + 2 * d) % row_count, col) for d in range(1, row_count // 2)]
    return row, col, core, (sibling, col), far, near, level


def greet(peers):
    barrier = pltpu.get_barrier_semaphore()
    for peer in peers:
        pl.semaphore_signal(barrier, inc=1, device_id=peer, device_id_type=MESH)
    pl.semaphore_wait(barrier, len(peers))


def remote(source, target, send_sem, recv_sem, peer):
    return pltpu.make_async_remote_copy(
        src_ref=source,
        dst_ref=target,
        send_sem=send_sem,
        recv_sem=recv_sem,
        device_id=peer,
        device_id_type=MESH,
    )


def relay(parts, count, place, far_sem, near_sem, side_sem, recv_sem, pair=True, between=None):
    row, col, core, sibling, far, near, _ = place
    outer, inner = len(far) + 1, len(near) + 1
    home, lane = col // inner, col % inner
    started = []

    def send(part, block, sem, peer, valid=None):
        def build():
            ref = parts(core, block)[part]
            return remote(ref, ref, sem, recv_sem.at[part, core, block], peer)

        started.append((build, valid))
        if valid is None:
            build().start()
        else:
            pl.when(valid)(lambda: build().start())

    def arrived(part, which, block, valid=None):
        def wait():
            ref = parts(which, block)[part]
            sem = recv_sem.at[part, which, block]
            remote(ref, ref, side_sem.at[part, 0], sem, sibling).wait_recv()

        if valid is None:
            wait()
        else:
            pl.when(valid)(wait)

    def both(one, other):
        return one if other is None else jnp.logical_and(one, other)

    def onward(part, block, step, sign, valid=None):
        target = home + sign
        reached = jnp.logical_and(target >= 0, target < outer)
        peer = (row, jnp.clip(target, 0, outer - 1) * inner + lane)
        send(part, block, far_sem.at[part, step], peer, both(reached, valid))

    def pass_on(part, block, step, valid=None):
        for e, peer in enumerate(near):
            send(part, block, near_sem.at[part, step, e], peer, valid)
        if pair:
            send(part, block, side_sem.at[part, step], sibling, valid)

    for part in range(count):
        onward(part, col, 0, -1)
        onward(part, col, 1, 1)
        pass_on(part, col, 0)
    if between is not None:
        between()
    for d in range(1, outer):
        for turn, sign in enumerate((-1, 1)):
            source = home + sign * d
            valid = jnp.logical_and(source >= 0, source < outer)
            block = jnp.clip(source, 0, outer - 1) * inner + lane
            for part in range(count):
                arrived(part, core, block, valid)
                onward(part, block, 2 * d + turn, -sign, valid)
                pass_on(part, block, 2 * d + turn, valid)
    for d in range(outer):
        for e in range(1, inner):
            block = ((home + d) % outer) * inner + (lane + e) % inner
            for part in range(count):
                arrived(part, core, block)
                if pair:
                    send(part, block, side_sem.at[part, 2 * outer + e * outer + d], sibling)
    if pair:
        for block in range(outer * inner):
            for part in range(count):
                arrived(part, 1 - core, block)
    for build, valid in started:
        if valid is None:
            build().wait_send()
        else:
            pl.when(valid)(lambda build=build: build().wait_send())


def relay_sems(count, col_count):
    outer, inner = split_axis(col_count)
    return [
        pltpu.SemaphoreType.DMA((count, 2 * outer)),
        pltpu.SemaphoreType.DMA((count, 2 * outer, inner)),
        pltpu.SemaphoreType.DMA((count, 2 * outer + col_count)),
        pltpu.SemaphoreType.DMA((count, 2, col_count)),
    ]


def gather_kernel(
    row_count, col_count, panel_ref, trail_ref, all_ref, own_sem, *sems
):
    place = here_and_peers(row_count, col_count)
    row, col, core, sibling, far, near, _ = place
    panel_width, trail_width = panel_ref.shape[0], trail_ref.shape[0]
    half = panel_ref.shape[1] // 2

    def lanes(which):
        return pl.ds(pl.multiple_of(which * half, half), half)

    def parts(which, block):
        panel_rows = pl.ds(pl.multiple_of(block * panel_width, panel_width), panel_width)
        first = col_count * panel_width + block * trail_width
        trail_rows = pl.ds(pl.multiple_of(first, panel_width), trail_width)
        return [all_ref.at[panel_rows, lanes(which)], all_ref.at[trail_rows, lanes(which)]]

    own = parts(core, col)
    copies = [
        pltpu.make_async_copy(panel_ref.at[:, lanes(core)], own[0], own_sem.at[0]),
        pltpu.make_async_copy(trail_ref.at[:, lanes(core)], own[1], own_sem.at[1]),
    ]
    for copy in copies:
        copy.start()
    greet([sibling, *far, *near])
    for copy in copies:
        copy.wait()
    relay(parts, 2, place, *sems)


def gather_environments(sparse_panel, sparse_trail, row_count, col_count):
    depth = sparse_panel.shape[1]
    width = sparse_panel.shape[0] + sparse_trail.shape[0]
    return pl.pallas_call(
        lambda *refs: gather_kernel(row_count, col_count, *refs),
        out_shape=jax.ShapeDtypeStruct((col_count * width, depth), sparse_panel.dtype),
        in_specs=[VMEM_SPEC] * 2,
        out_specs=VMEM_SPEC,
        scratch_shapes=[pltpu.SemaphoreType.DMA((2,)), *relay_sems(2, col_count)],
        compiler_params=pltpu.CompilerParams(
            collective_id=1, has_side_effects=True, vmem_limit_bytes=32 * 1024 * 1024
        ),
        name="gather_environments",
    )(sparse_panel, sparse_trail)


def exchange_kernel(
    row_count,
    col_count,
    rows_ref,
    panel_ref,
    trail_ref,
    held_ref,
    own_sem,
    row_send,
    row_recv,
    trail_send,
    trail_recv,
    *sems,
):
    place = here_and_peers(row_count, col_count)
    row, col, core, sibling, far, near, _ = place
    panel_total = panel_ref.shape[1]
    trail_width = trail_ref.shape[1]
    slots = rows_ref.shape[0] // row_count
    wide = held_ref.shape[0]
    groups = [(row + d) % row_count for d in range(1, row_count)]
    others = [(col + d) % col_count for d in range(1, col_count)]
    sides = [slice(0, panel_total), slice(panel_total, rows_ref.shape[1])]

    def slot_range(group):
        return pl.ds(pl.multiple_of(group * slots, slots), slots)

    def wide_range(block):
        return pl.ds(pl.multiple_of(block * wide, wide), wide)

    own = pltpu.make_async_copy(
        rows_ref.at[slot_range(row)], held_ref.at[slot_range(row)], own_sem.at[0]
    )
    own.start()
    greet([(group, col) for group in groups] + [(row, other) for other in others])
    started = []

    def send(source, target, send_sem, recv_sem, peer):
        copy = remote(source, target, send_sem, recv_sem, peer)
        copy.start()
        started.append(copy)

    def arrived(target, recv_sem):
        remote(target, target, row_send.at[0, 0], recv_sem, sibling).wait_recv()

    for side, lanes in enumerate(sides):
        for d, group in enumerate(groups):
            send(
                rows_ref.at[slot_range(group), lanes],
                held_ref.at[slot_range(row), lanes],
                row_send.at[side, d],
                row_recv.at[side, row],
                (group, col),
            )
    own.wait()
    for group in groups:
        arrived(held_ref.at[slot_range(group), sides[0]], row_recv.at[0, group])
    mine = held_ref.at[:, sides[0]]
    keep = pltpu.make_async_copy(mine, panel_ref.at[wide_range(col)], own_sem.at[1])
    keep.start()
    keep.wait()

    def trail_lanes(block):
        first = panel_total + block * trail_width
        return pl.ds(pl.multiple_of(first, trail_width), trail_width)

    keep_trail = pltpu.make_async_copy(
        held_ref.at[:, trail_lanes(col)], trail_ref.at[wide_range(col)], own_sem.at[2]
    )

    def send_trail():
        for group in groups:
            arrived(held_ref.at[slot_range(group), sides[1]], row_recv.at[1, group])
        for d, other in enumerate(others):
            send(
                held_ref.at[:, trail_lanes(other)],
                trail_ref.at[wide_range(col)],
                trail_send.at[d],
                trail_recv.at[col],
                (row, other),
            )
        keep_trail.start()

    def parts(which, block):
        return [panel_ref.at[wide_range(block)]]

    relay(parts, 1, place, *sems, pair=False, between=send_trail)
    for other in others:
        arrived(trail_ref.at[wide_range(other)], trail_recv.at[other])
    keep_trail.wait()
    for copy in started:
        copy.wait_send()


def exchange_rows(kernel_rows, panel_total, row_count, col_count):
    total, env_count = kernel_rows.shape
    trail_width = (env_count - panel_total) // col_count
    return pl.pallas_call(
        lambda *refs: exchange_kernel(row_count, col_count, *refs),
        out_shape=(
            jax.ShapeDtypeStruct((total * col_count, panel_total), kernel_rows.dtype),
            jax.ShapeDtypeStruct((total * col_count, trail_width), kernel_rows.dtype),
        ),
        in_specs=[VMEM_SPEC],
        out_specs=(VMEM_SPEC, VMEM_SPEC),
        scratch_shapes=[
            pltpu.VMEM((total, env_count), kernel_rows.dtype),
            pltpu.SemaphoreType.DMA((3,)),
            pltpu.SemaphoreType.DMA((2, row_count)),
            pltpu.SemaphoreType.DMA((2, row_count)),
            pltpu.SemaphoreType.DMA((col_count,)),
            pltpu.SemaphoreType.DMA((col_count,)),
            *relay_sems(1, col_count),
        ],
        compiler_params=pltpu.CompilerParams(
            collective_id=3, has_side_effects=True, vmem_limit_bytes=40 * 1024 * 1024
        ),
        name="exchange_rows",
    )(kernel_rows)


def sum_kernel(
    row_count,
    col_count,
    gram_part,
    cross_part,
    gram_ref,
    cross_ref,
    side_ref,
    level_ref,
    side_send,
    side_recv,
    level_send,
    level_recv,
    cross_send,
    cross_recv,
    *sems,
):
    place = here_and_peers(row_count, col_count)
    row, col, core, sibling, far, near, level = place
    gram_half = gram_part.shape[0] // 2
    cross_half = cross_part.shape[0] // 2
    greet([sibling, *far, *near, *level])

    def gram_rows(which):
        return pl.ds(pl.multiple_of(which * gram_half, gram_half), gram_half)

    def cross_rows(which):
        return pl.ds(pl.multiple_of(which * cross_half, cross_half), cross_half)

    to_side = [
        remote(
            gram_part.at[gram_rows(1 - core)],
            side_ref.at[:gram_half],
            side_send.at[0],
            side_recv.at[0],
            sibling,
        ),
        remote(
            cross_part.at[cross_rows(1 - core)],
            side_ref.at[gram_half:],
            side_send.at[1],
            side_recv.at[1],
            sibling,
        ),
    ]
    for copy in to_side:
        copy.start()
    for copy in to_side:
        copy.wait()
    floor = row // 2
    level_ref[floor, :gram_half] = gram_part[gram_rows(core), :] + side_ref[:gram_half]
    level_ref[floor, gram_half:] = cross_part[cross_rows(core), :] + side_ref[gram_half:]
    to_level = []
    for d, peer in enumerate(level):
        mine = level_ref.at[floor]
        copy = remote(mine, mine, level_send.at[d], level_recv.at[floor], peer)
        copy.start()
        to_level.append(copy)
    for d, peer in enumerate(level):
        other = peer[0] // 2
        theirs = level_ref.at[other]
        remote(theirs, theirs, level_send.at[d], level_recv.at[other], peer).wait_recv()
    total = level_ref[0]
    for other in range(1, row_count // 2):
        total = total + level_ref[other]

    def parts(which, block):
        first = block * (2 * gram_half) + which * gram_half
        return [gram_ref.at[pl.ds(pl.multiple_of(first, gram_half), gram_half)]]

    parts(core, col)[0][...] = total[:gram_half]
    cross_ref[cross_rows(core), :] = total[gram_half:]
    mine = cross_ref.at[cross_rows(core)]
    to_cross = remote(mine, mine, cross_send.at[0], cross_recv.at[0], sibling)
    to_cross.start()
    relay(parts, 1, place, *sems)
    to_cross.wait()
    for copy in to_level:
        copy.wait_send()


def sum_products(gram_part, cross_part, row_count, col_count):
    width = gram_part.shape[1]
    half = (gram_part.shape[0] + cross_part.shape[0]) // 2
    levels = row_count // 2
    return pl.pallas_call(
        lambda *refs: sum_kernel(row_count, col_count, *refs),
        out_shape=(
            jax.ShapeDtypeStruct((gram_part.shape[0] * col_count, width), jnp.float32),
            jax.ShapeDtypeStruct(cross_part.shape, jnp.float32),
        ),
        in_specs=[VMEM_SPEC] * 2,
        out_specs=(VMEM_SPEC, VMEM_SPEC),
        scratch_shapes=[
            pltpu.VMEM((half, width), jnp.float32),
            pltpu.VMEM((levels, half, width), jnp.float32),
            pltpu.SemaphoreType.DMA((2,)),
            pltpu.SemaphoreType.DMA((2,)),
            pltpu.SemaphoreType.DMA((levels,)),
            pltpu.SemaphoreType.DMA((levels,)),
            pltpu.SemaphoreType.DMA((1,)),
            pltpu.SemaphoreType.DMA((1,)),
            *relay_sems(1, col_count),
        ],
        compiler_params=pltpu.CompilerParams(
            collective_id=2, has_side_effects=True, vmem_limit_bytes=32 * 1024 * 1024
        ),
        name="sum_products",
    )(gram_part, cross_part)


def contract_rows(left_side, right_side):
    return lax.dot_general(
        left_side, right_side, (((1,), (1,)), ((), ())), preferred_element_type=jnp.float32
    )


def contract_cols(left_side, right_side):
    return lax.dot_general(
        left_side, right_side, (((0,), (0,)), ((), ())), preferred_element_type=jnp.float32
    )


def project(weights, segment):
    return lax.dot_general(
        weights, segment, (((0,), (1,)), ((), ())), preferred_element_type=jnp.float32
    )


def per_device(
    descriptors, gradients, sparse_panel, sparse_trail, atom_counts, owner_rows, neighbor_ids
):
    row_count = lax.axis_size("row")
    col_count = lax.axis_size("col")
    count_here = atom_counts[0]
    owner_here = owner_rows[0]
    slope_here = gradients.reshape(-1, gradients.shape[3])
    panel_width = sparse_panel.shape[0]
    panel_total = panel_width * col_count
    slot_count = 4 * neighbor_ids.shape[1]
    total_rows = row_count * row_count * col_count * slot_count
    environments = gather_environments(sparse_panel, sparse_trail, row_count, col_count)
    kernel_rows = slot_rows(
        environments, descriptors, slope_here, count_here, neighbor_ids, owner_here
    )
    segment, trail_own = exchange_rows(kernel_rows, panel_total, row_count, col_count)
    first = lax.axis_index("col") * panel_width
    panel_own = lax.dynamic_slice_in_dim(segment, first, panel_width, 1)
    gram_sum, cross_sum = sum_products(
        contract_cols(panel_own, segment), contract_cols(trail_own, segment), row_count, col_count
    )
    panel_factor, cross_factor, weight_high, weight_low = factor_panel(
        gram_sum, cross_sum, total_rows
    )
    trail_residual = (
        trail_own.T.astype(jnp.float32)
        - project(weight_high, segment)
        - project(weight_low, segment)
    )
    return (panel_factor, cross_factor, trail_residual)


def solution(mesh):
    return jax.shard_map(
        per_device,
        mesh=mesh,
        in_specs=(
            P(("row", "col"), None),
            P(None, None, ("row", "col"), None),
            P("col", None),
            P("col", None),
            P(("row", "col"), None),
            P(("row", "col"), None),
            P(("row", "col"), None, None),
        ),
        out_specs=(P(), P("col", None), P("col", "row")),
        check_vma=False,
    )
```
